32 devices in a mesh: seq: 4 (over z), fsdp: 8 (over y, x, core).
Axes of the slice: x: 2, y: 2, z: 4, core: 2. Of those that a mesh axis runs over, the one named last changes fastest.
Arguments:
- frames: bfloat16 [8, 1024, 1536], P('fsdp', 'seq'), may hold values from -6 to 6
- conv_kernel: float32 [31, 1536], replicated, may hold values from -1 to 1
- pw_weight: bfloat16 [1536, 1536], P('fsdp'), may hold values from -0.15625 to 0.15625
- head_weight: bfloat16 [1536, 8192], P(None, 'fsdp'), may hold values from -4.5 to 4.5
- targets: int32 [8, 1024], P('fsdp', 'seq'), may hold values from 0 to 8191
- frame_weight: bfloat16 [8, 1024], P('fsdp', 'seq'), may hold values from 0.19921875 to 1
Outputs:
- frames_grad: bfloat16 [8, 1024, 1536], P('fsdp', 'seq')
- kernel_grad: float32 [31, 1536], replicated
- pw_grad: float32 [1536, 1536], P(('seq', 'fsdp'))
- head_grad: float32 [1536, 8192], P('seq', 'fsdp')
The draws below stay inside these ranges and needn't reach their ends.
All inputs are finite; a program needn't handle non-finite values.
Results may differ from the reference program's by a relative error of at most 0.014.
The reference program's roundings to bfloat16 on the way (of `gated`, `mixed`, `dlogits`, `dmixed` and `dconv`) count: a program that leaves them out, or rounds other values in their place, can miss the bound.
Values may be sent and summed in bfloat16 or wider, within the bound.
No kernel may reach another device: no remote copies, remote signals or barrier semaphores. Data moves between devices by JAX's collectives and lax.ppermute only.
A program may use at most 128 MiB of HBM per device.

```python
import math
import jax
import jax.numpy as jnp
from jax import lax

D = 1536
V = 8192
K = 31
B = 8
L = 1024
N_FSDP = 8


def draw_head_weight(key, part):
    key = jax.random.fold_in(key, 7)
    spread = 2.8 / math.sqrt(D)
    base = jnp.clip(jax.random.normal(key, (D, V), jnp.float32), -5.0, 5.0)
    return (base * spread).astype(jnp.bfloat16)


def set_ends(drawn, stream_key, low, top_value):
    spot = [jax.random.randint(jax.random.fold_in(stream_key, axis), (), 0, length) for axis, length in enumerate(drawn.shape)]
    widest = drawn.shape.index(max(drawn.shape))
    neighbour = spot[:widest] + [(spot[widest] + 1) % drawn.shape[widest]] + spot[widest + 1:]
    return drawn.at[tuple(spot)].set(low).at[tuple(neighbour)].set(top_value)


def steps_of(key, shape, cuts, low, top_value):
    level, own = 1.0, jax.random.fold_in(key, 6)
    for position, blocks in cuts:
        draws = jnp.exp(jax.random.uniform(jax.random.fold_in(own, position), (blocks,), jnp.float32, low / len(cuts), top_value / len(cuts)))
        level = level * jnp.repeat(draws, shape[position] // blocks).reshape([-1 if axis == position else 1 for axis in range(len(shape))])
    return level


def normal_values(own_key, shape, deviation, most, shards=(), held_as=jnp.bfloat16):
    entries = deviation * jax.random.normal(own_key, shape, jnp.float32)
    if shards:
        entries = entries * steps_of(own_key, shape, shards, -0.22, 0.18)
    return jnp.clip(entries, -most, most).astype(held_as)


def setup_inputs(seed: int = 0) -> dict:
    splits = jax.random.split(jax.random.key(seed), 7)
    frames = normal_values(splits[0], (B, L, D), 1.0, 6.0, ((0, 8), (1, 4)))
    conv_kernel = normal_values(splits[1], (K, D), K ** -0.5, 1.0, (), jnp.float32)
    pw_weight = normal_values(splits[2], (D, D), D ** -0.5, 0.15625, ((0, 8),))
    head_weight = draw_head_weight(jax.random.fold_in(splits[6], 71), 0)
    targets = set_ends(jax.random.randint(splits[4], (B, L), 0, V), jax.random.fold_in(splits[4], 1), 0, V - 1).astype(jnp.int32)
    frame_weight = jnp.clip(jnp.exp(math.log(1.0) - 1.6133518 * jax.random.uniform(splits[5], (B, L), jnp.float32) ** steps_of(splits[5], (B, L), ((0, 8), (1, 4)), -0.2, 0.2)), 0.19921875, 1.0).astype(jnp.bfloat16)
    return {"frames": frames, "conv_kernel": conv_kernel, "pw_weight": pw_weight, "head_weight": head_weight, "targets": targets, "frame_weight": frame_weight}


def one_utterance(frames_b, targets_b, weight_b, conv_kernel, pw_weight, head_weight):
    reach = (K - 1) // 2
    length = frames_b.shape[0]
    padded = jnp.pad(frames_b, ((reach, reach), (0, 0))).astype(jnp.float32)
    conv = jnp.zeros((length, D), jnp.float32)
    for tap in range(K):
        conv = conv + conv_kernel[tap] * padded[tap:tap + length]
    gated = jax.nn.silu(conv).astype(jnp.bfloat16)
    proj = jnp.dot(gated, pw_weight, preferred_element_type=jnp.float32)
    mixed = (frames_b.astype(jnp.float32) + proj).astype(jnp.bfloat16)
    logits = jnp.dot(mixed, head_weight, preferred_element_type=jnp.float32)
    top = jnp.max(logits, axis=1, keepdims=True)
    expo = jnp.exp(logits - top)
    probs = expo / jnp.sum(expo, axis=1, keepdims=True)
    hit = (targets_b[:, None] == jnp.arange(V, dtype=jnp.int32)[None, :]).astype(jnp.float32)
    dlogits = (weight_b.astype(jnp.float32)[:, None] * (probs - hit)).astype(jnp.bfloat16)
    head_term = lax.dot_general(mixed, dlogits, (((0,), (0,)), ((), ())), preferred_element_type=jnp.float32)
    block = V // N_FSDP
    dl_blocks = dlogits.reshape(length, N_FSDP, block).transpose(1, 0, 2)
    hw_blocks = head_weight.reshape(D, N_FSDP, block).transpose(1, 0, 2)

    def add_block(total, pair):
        part = lax.dot_general(pair[0], pair[1], (((1,), (1,)), ((), ())), preferred_element_type=jnp.float32)
        part = lax.optimization_barrier(part.astype(jnp.bfloat16))
        return total + part.astype(jnp.float32), None

    dsum, _ = lax.scan(add_block, jnp.zeros((length, D), jnp.float32), (dl_blocks, hw_blocks))
    dmixed = dsum.astype(jnp.bfloat16)
    pw_term = lax.dot_general(gated, dmixed, (((0,), (0,)), ((), ())), preferred_element_type=jnp.float32)
    dgated = lax.dot_general(dmixed, pw_weight, (((1,), (1,)), ((), ())), preferred_element_type=jnp.float32)
    sig = jax.nn.sigmoid(conv)
    dconv = (dgated * sig * (1.0 + conv * (1.0 - sig))).astype(jnp.bfloat16)
    dpad = jnp.pad(dconv, ((reach, reach), (0, 0))).astype(jnp.float32)
    dconv_f = dconv.astype(jnp.float32)
    kernel_rows = []
    back = dmixed.astype(jnp.float32)
    for tap in range(K):
        kernel_rows.append(jnp.sum(dconv_f * padded[tap:tap + length], axis=0))
        back = back + conv_kernel[tap] * dpad[2 * reach - tap:2 * reach - tap + length]
    kernel_term = jnp.stack(kernel_rows, axis=0)
    return back.astype(jnp.bfloat16), kernel_term, pw_term, head_term


def reference(frames, conv_kernel, pw_weight, head_weight, targets, frame_weight):
    def step(carry, items):
        grad_b, kernel_term, pw_term, head_term = one_utterance(items[0], items[1], items[2], conv_kernel, pw_weight, head_weight)
        return (carry[0] + kernel_term, carry[1] + pw_term, carry[2] + head_term), grad_b

    start = (jnp.zeros((K, D), jnp.float32), jnp.zeros((D, D), jnp.float32), jnp.zeros((D, V), jnp.float32))
    sums, frames_grad = lax.scan(step, start, (frames, targets, frame_weight))
    return frames_grad, sums[0], sums[1], sums[2]
```

```python
import jax
import jax.numpy as jnp
from jax import lax
from jax.sharding import PartitionSpec as P

BF = jnp.bfloat16
F32 = jnp.float32


def swap(value, mask):
    count = lax.axis_size("fsdp")
    return lax.ppermute(value, "fsdp", [(i, i ^ mask) for i in range(count)])


def gather_chips(block):
    chips = lax.axis_size("fsdp") // 2
    if chips != 4:
        return [block] + [swap(block, 2 * m) for m in range(1, chips)]
    half = block.shape[0] // 2
    from_x = swap(block, 2)
    from_y = swap(block, 4)
    far_low = swap(from_x[:half], 4)
    far_high = swap(from_y[half:], 2)
    return [block, from_x, from_y, jnp.concatenate([far_low, far_high], axis=0)]


def scatter_chips(parts):
    chips = len(parts)
    if chips != 4:
        total = parts[0]
        for m in range(1, chips):
            total = total + swap(parts[m].astype(BF), 2 * m).astype(F32)
        return total
    half = parts[0].shape[0] // 2
    far = parts[3].astype(BF)
    low = swap(far[:half], 2).astype(F32)
    high = swap(far[half:], 4).astype(F32)
    to_y = jnp.concatenate([parts[2][:half] + low, parts[2][half:]], axis=0).astype(BF)
    to_x = jnp.concatenate([parts[1][:half], parts[1][half:] + high], axis=0).astype(BF)
    return parts[0] + swap(to_x, 2).astype(F32) + swap(to_y, 4).astype(F32)


def line_scatter(term, kind):
    count = lax.axis_size("seq")
    here = lax.axis_index("seq")

    def block(index):
        index = jnp.clip(index, 0, count - 1)
        return lax.dynamic_index_in_dim(term, index, 0, keepdims=False).astype(F32)

    up = down = None
    for step in range(1, count):
        to_up = block(here + count - step)
        to_down = block(here - count + step)
        if up is not None:
            to_up = to_up + up.astype(F32)
            to_down = to_down + down.astype(F32)
        up = lax.ppermute(to_up.astype(kind), "seq", [(i, i + 1) for i in range(step)])
        down = lax.ppermute(
            to_down.astype(kind), "seq", [(i, i - 1) for i in range(count - step, count)]
        )
    return block(here) + up.astype(F32) + down.astype(F32)


def halo(block, width):
    count = lax.axis_size("seq")
    forward = [(i, i + 1) for i in range(count - 1)]
    backward = [(i + 1, i) for i in range(count - 1)]
    low = lax.ppermute(block[block.shape[0] - width :], "seq", forward)
    high = lax.ppermute(block[:width], "seq", backward)
    return jnp.concatenate([low, block, high], axis=0)


def body(frames, conv_kernel, pw_weight, head_weight, targets, frame_weight):
    frames = frames[0]
    rows, width = frames.shape
    taps = conv_kernel.shape[0]
    reach = (taps - 1) // 2
    seqs = lax.axis_size("seq")
    count = lax.axis_size("fsdp")
    chips = count // 2
    me = lax.axis_index("fsdp")
    chip = me // 2
    core = me % 2
    padded = halo(frames, reach)
    labels = jnp.stack([targets[0].astype(F32), frame_weight[0].astype(F32)])
    all_labels = [labels] + [swap(labels, 2 * m) for m in range(1, chips)]
    pw_mine = gather_chips(pw_weight)
    pw_other = swap(jnp.stack(pw_mine), 1)
    shard = pw_weight.shape[0]
    pw_full = jnp.zeros((count, shard, width), BF)
    for m in range(chips):
        pw_full = lax.dynamic_update_index_in_dim(pw_full, pw_mine[m], me ^ (2 * m), 0)
        pw_full = lax.dynamic_update_index_in_dim(pw_full, pw_other[m], me ^ (2 * m + 1), 0)
    pw_full = pw_full.reshape(width, width)
    head_other = swap(head_weight, 1)

    conv = jnp.zeros((rows, width), F32)
    for tap in range(taps):
        conv = conv + conv_kernel[tap] * padded[tap : tap + rows].astype(F32)
    gated = jax.nn.silu(conv).astype(BF)
    proj = jnp.dot(gated, pw_full, preferred_element_type=F32)
    mixed = (frames.astype(F32) + proj).astype(BF)

    all_mixed = gather_chips(mixed)
    piece = width // (seqs * count)
    gated_t = gated.T.reshape(seqs, chips, 2, piece, rows)
    gated_t = jnp.stack(
        [lax.dynamic_index_in_dim(gated_t, chip ^ m, 1, keepdims=False) for m in range(chips)]
    )
    gated_own = lax.dynamic_index_in_dim(gated_t, core, 2, keepdims=False)
    gated_sent = lax.dynamic_index_in_dim(gated_t, 1 - core, 2, keepdims=False)
    gated_got = swap(gated_sent, 1)
    gated_pair = jnp.concatenate([gated_own, gated_got], axis=-1)

    weights = (head_weight, head_other)
    vocab = head_weight.shape[1]
    logits = []
    stats = []
    for m in range(chips):
        pair = [jnp.dot(all_mixed[m], w, preferred_element_type=F32) for w in weights]
        top = jnp.maximum(jnp.max(pair[0], axis=1), jnp.max(pair[1], axis=1))
        total = sum(jnp.sum(jnp.exp(l - top[:, None]), axis=1) for l in pair)
        logits.append(pair)
        stats.append((top, total))
    mixed_other = swap(jnp.stack(all_mixed), 1)
    tops = jnp.stack([s[0] for s in stats])
    totals = jnp.stack([s[1] for s in stats])
    packed = jnp.concatenate([tops, totals], axis=0)
    got = [packed] + [swap(packed, 2 * m) for m in range(1, chips)]
    dl_own, dl_other = [], []
    entries = lax.broadcasted_iota(jnp.int32, (1, vocab), 1)
    for m in range(chips):
        part_tops = [got[o][m ^ o] for o in range(chips)]
        part_totals = [got[o][chips + (m ^ o)] for o in range(chips)]
        top = part_tops[0]
        for t in part_tops[1:]:
            top = jnp.maximum(top, t)
        total = sum(s * jnp.exp(t - top) for s, t in zip(part_totals, part_tops))
        inverse = 1.0 / total
        target = all_labels[m][0].astype(jnp.int32)
        weight = all_labels[m][1]
        for l, owner, into in ((logits[m][0], me, dl_own), (logits[m][1], me ^ 1, dl_other)):
            hit = ((target - owner * vocab)[:, None] == entries).astype(F32)
            probs = jnp.exp(l - top[:, None]) * inverse[:, None]
            into.append((weight[:, None] * (probs - hit)).astype(BF))
    dl_got = swap(jnp.stack(dl_other), 1)

    def back_head(m):
        rhs = (((1,), (1,)), ((), ()))
        return lax.dot_general(
            dl_own[m], head_weight, rhs, preferred_element_type=F32
        ) + lax.dot_general(dl_other[m], head_other, rhs, preferred_element_type=F32)

    dmixed = scatter_chips([back_head(m) for m in range(chips)]).astype(BF)

    left = jnp.concatenate([jnp.concatenate(all_mixed, 0), mixed_other.reshape(-1, width)], 0)
    right = jnp.concatenate([jnp.concatenate(dl_own, 0), dl_got.reshape(-1, vocab)], 0)
    head_term = lax.dot_general(
        left, right, (((0,), (0,)), ((), ())), preferred_element_type=F32
    )
    head_grad = line_scatter(head_term.reshape(seqs, width // seqs, vocab), BF)

    dmixed_pair = jnp.concatenate([dmixed, swap(dmixed, 1)], axis=0)
    pw_term = jnp.dot(
        gated_pair.reshape(-1, 2 * rows), dmixed_pair, preferred_element_type=F32
    ).reshape(chips, seqs * piece, width)
    pw_sum = scatter_chips([pw_term[m] for m in range(chips)])
    pw_grad = line_scatter(pw_sum.reshape(seqs, piece, width), BF)

    dgated = lax.dot_general(
        dmixed, pw_full, (((1,), (1,)), ((), ())), preferred_element_type=F32
    )
    sig = jax.nn.sigmoid(conv)
    dconv = (dgated * sig * (1.0 + conv * (1.0 - sig))).astype(BF)
    dpad = halo(dconv, reach)
    dconv_f = dconv.astype(F32)
    back = dmixed.astype(F32)
    kernel_rows = []
    for tap in range(taps):
        kernel_rows.append(jnp.sum(dconv_f * padded[tap : tap + rows].astype(F32), axis=0))
        back = back + conv_kernel[tap] * dpad[2 * reach - tap : 2 * reach - tap + rows].astype(F32)
    kernel_grad = jnp.stack(kernel_rows, axis=0)
    mask = 1
    while mask < count:
        kernel_grad = kernel_grad + swap(kernel_grad, mask)
        mask *= 2
    mask = 1
    while mask < seqs:
        kernel_grad = kernel_grad + lax.ppermute(
            kernel_grad, "seq", [(i, i ^ mask) for i in range(seqs)]
        )
        mask *= 2
    return (back.astype(BF)[None], kernel_grad, pw_grad, head_grad)


def solution(mesh):
    return jax.shard_map(
        body,
        mesh=mesh,
        in_specs=(
            P("fsdp", "seq", None),
            P(),
            P("fsdp", None),
            P(None, "fsdp"),
            P("fsdp", "seq"),
            P("fsdp", "seq"),
        ),
        out_specs=(P("fsdp", "seq", None), P(), P(("seq", "fsdp"), None), P("seq", "fsdp")),
        check_vma=False,
    )
```

```python
import jax
import jax.numpy as jnp
from jax import lax
from jax.experimental import pallas as pl
from jax.experimental.pallas import tpu as pltpu
from jax.sharding import PartitionSpec as P

BF = jnp.bfloat16
F32 = jnp.float32


def swap(value, mask):
    count = lax.axis_size("fsdp")
    return lax.ppermute(value, "fsdp", [(i, i ^ mask) for i in range(count)])


VMEM_BYTES = 56 * 2**20
CHEAP = pl.CostEstimate(flops=0, bytes_accessed=0, transcendentals=0)


def halves_to_forward(from_x, from_y, *earlier):
    rows, width = from_x.shape
    half = rows // 2

    def kernel(x_ref, y_ref, *refs):
        low_ref, high_ref = refs[len(earlier) :]
        low_ref[...] = x_ref[...]
        high_ref[...] = y_ref[...]

    made = jax.ShapeDtypeStruct((half, width), from_x.dtype)
    whole = pl.BlockSpec((half, width), lambda j: (0, 0))
    return pl.pallas_call(
        kernel,
        grid=(1,),
        out_shape=(made, made),
        in_specs=[
            pl.BlockSpec((half, width), lambda j: (0, 0)),
            pl.BlockSpec((half, width), lambda j: (1, 0)),
        ]
        + [pl.BlockSpec(memory_space=pl.ANY)] * len(earlier),
        out_specs=(whole, whole),
        compiler_params=pltpu.CompilerParams(vmem_limit_bytes=VMEM_BYTES),
        cost_estimate=CHEAP,
        name="forward",
    )(from_x, from_y, *earlier)


def near_and_forward(block, from_x, from_y, *earlier):
    rows, width = block.shape
    half = rows // 2

    def kernel(own_ref, x_ref, y_ref, *refs):
        near_ref, low_ref, high_ref = refs[len(earlier) :]
        near_ref[:rows, :] = own_ref[...]
        near_ref[rows : 2 * rows, :] = x_ref[...]
        near_ref[2 * rows :, :] = y_ref[...]
        low_ref[...] = x_ref[:half, :]
        high_ref[...] = y_ref[half:, :]

    def spec(count):
        return pl.BlockSpec((count, width), lambda j: (0, 0))

    made = jax.ShapeDtypeStruct((half, width), block.dtype)
    return pl.pallas_call(
        kernel,
        grid=(1,),
        out_shape=(jax.ShapeDtypeStruct((3 * rows, width), block.dtype), made, made),
        in_specs=[spec(rows)] * 3 + [pl.BlockSpec(memory_space=pl.ANY)] * len(earlier),
        out_specs=(spec(3 * rows), spec(half), spec(half)),
        compiler_params=pltpu.CompilerParams(vmem_limit_bytes=VMEM_BYTES),
        cost_estimate=CHEAP,
        name="near_and_forward",
    )(block, from_x, from_y, *earlier)


def stack_halves(low, high, *earlier):
    half, width = low.shape

    def kernel(low_ref, high_ref, *refs):
        refs[-1][:half, :] = low_ref[...]
        refs[-1][half:, :] = high_ref[...]

    part = pl.BlockSpec((half, width), lambda j: (0, 0))
    return pl.pallas_call(
        kernel,
        grid=(1,),
        out_shape=jax.ShapeDtypeStruct((2 * half, width), low.dtype),
        in_specs=[part, part] + [pl.BlockSpec(memory_space=pl.ANY)] * len(earlier),
        out_specs=pl.BlockSpec((2 * half, width), lambda j: (0, 0)),
        compiler_params=pltpu.CompilerParams(vmem_limit_bytes=VMEM_BYTES),
        cost_estimate=CHEAP,
        name="stack_halves",
    )(low, high, *earlier)


def gather_rows(block, earlier, between):
    chips = lax.axis_size("fsdp") // 2
    if chips != 4:
        near = jnp.concatenate([block] + [swap(block, 2 * m) for m in range(1, chips - 1)])
        between(near)
        return near, swap(block, 2 * (chips - 1))
    near, to_y, to_x = near_and_forward(block, swap(block, 2), swap(block, 4), *earlier)
    low = swap(to_y, 4)
    high = swap(to_x, 2)
    return near, stack_halves(low, high, *between(near))


def join_halves(near_y, near_x, low, high, earlier, passed=()):
    half, width = low.shape
    rows = 2 * half
    tile = 512 if width % 512 == 0 else width
    count = len(passed)

    def kernel(y_ref, x_ref, low_ref, high_ref, *refs):
        to_y_ref, to_x_ref = refs[len(earlier) + count : len(earlier) + count + 2]
        to_y_ref[:half, :] = (y_ref[:half, :] + low_ref[...].astype(F32)).astype(BF)
        to_y_ref[half:, :] = y_ref[half:, :].astype(BF)
        to_x_ref[:half, :] = x_ref[:half, :].astype(BF)
        to_x_ref[half:, :] = (x_ref[half:, :] + high_ref[...].astype(F32)).astype(BF)
        for n in range(count):
            refs[len(earlier) + count + 2 + n][...] = refs[n][...]

    def block(size, index):
        return pl.BlockSpec((size, tile), lambda j: (index, j))

    made = jax.ShapeDtypeStruct((rows, width), BF)
    return pl.pallas_call(
        kernel,
        grid=(width // tile,),
        out_shape=(made, made)
        + tuple(jax.ShapeDtypeStruct((size, width), value.dtype) for value, size, _ in passed),
        in_specs=[block(rows, near_y[1]), block(rows, near_x[1]), block(half, 0), block(half, 0)]
        + [block(size, index) for _, size, index in passed]
        + [pl.BlockSpec(memory_space=pl.ANY)] * len(earlier),
        out_specs=(block(rows, 0), block(rows, 0)) + tuple(block(size, 0) for _, size, _ in passed),
        compiler_params=pltpu.CompilerParams(vmem_limit_bytes=VMEM_BYTES),
        cost_estimate=CHEAP,
        name="join_halves",
    )(near_y[0], near_x[0], low, high, *[value for value, _, _ in passed], *earlier)


def gather_pieces(block, *earlier):
    chips = lax.axis_size("fsdp") // 2
    if chips != 4:
        return [(block, 0, 0)] + [(swap(block, 2 * m), m, 0) for m in range(1, chips)]
    half = block.shape[0] // 2
    from_x = swap(block, 2)
    from_y = swap(block, 4)
    if earlier:
        to_y, to_x = halves_to_forward(from_x, from_y, *earlier)
    else:
        to_y, to_x = from_x[:half], from_y[half:]
    far_low = swap(to_y, 4)
    far_high = swap(to_x, 2)
    return [(block, 0, 0), (from_x, 1, 0), (from_y, 2, 0), (far_low, 3, 0), (far_high, 3, half)]


def finish_sum(own, recv_x, recv_y, index, passed, dtype, *earlier):
    rows, width = recv_x.shape
    tile = 512 if width % 512 == 0 else width
    count = len(passed)

    def kernel(own_ref, x_ref, y_ref, *refs):
        outs = refs[count + len(earlier) :]
        total = own_ref[...] + x_ref[...].astype(F32) + y_ref[...].astype(F32)
        outs[0][...] = total.astype(dtype)
        for n in range(count):
            outs[1 + n][...] = refs[n][...]

    def block(size, at):
        return pl.BlockSpec((size, tile), lambda j: (at, j))

    return pl.pallas_call(
        kernel,
        grid=(width // tile,),
        out_shape=(jax.ShapeDtypeStruct((rows, width), dtype),)
        + tuple(jax.ShapeDtypeStruct(v.shape, v.dtype) for v in passed),
        in_specs=[block(rows, index), block(rows, 0), block(rows, 0)]
        + [block(v.shape[0], 0) for v in passed]
        + [pl.BlockSpec(memory_space=pl.ANY)] * len(earlier),
        out_specs=(block(rows, 0),) + tuple(block(v.shape[0], 0) for v in passed),
        compiler_params=pltpu.CompilerParams(vmem_limit_bytes=VMEM_BYTES),
        cost_estimate=CHEAP,
        name="finish_sum",
    )(own, recv_x, recv_y, *passed, *earlier)


def scatter_and_finish(part, near, chips, passed, last, dtype):
    if chips != 4:
        total = part(0)
        for m in range(1, chips):
            total = total + swap(part(m).astype(BF), 2 * m).astype(F32)
        kept = [v[size * index : size * (index + 1)] for v, size, index in passed]
        return total.astype(dtype), kept, last(kept, total)[0]
    far = part(3).astype(BF)
    half = far.shape[0] // 2
    low = swap(far[:half], 2)
    high = swap(far[half:], 4)
    own, index = near(0)
    to_y, to_x, *kept = join_halves(near(2), near(1), low, high, (own,), passed)
    recv_x, recv_y = swap(to_x, 2), swap(to_y, 4)
    handed, waited = last(kept, to_x)
    total, *handed = finish_sum(own, recv_x, recv_y, index, handed, dtype, *waited)
    return total, kept, handed


def project(gated, frames, pieces, places):
    rows, width = gated.shape
    count = len(pieces)
    tile = 512

    def kernel(*refs):
        place = refs[0]
        gated_ref, frames_ref = refs[1:3]
        piece_refs = refs[3 : 3 + count]
        mixed_ref, full_ref, held, sems, out_sem = refs[3 + count :]
        copies = []
        for n in range(count):
            size = piece_refs[n].shape[0]
            start = pl.multiple_of(place[n], 16)
            copy = pltpu.make_async_copy(piece_refs[n], held.at[pl.ds(start, size)], sems.at[n])
            copy.start()
            copies.append(copy)
        for copy in copies:
            copy.wait()
        out = pltpu.make_async_copy(held, full_ref, out_sem)
        out.start()
        for col in range(0, width, tile):
            at = slice(col, col + tile)
            proj = jnp.dot(gated_ref[...], held[:, at], preferred_element_type=F32)
            mixed_ref[:, at] = (frames_ref[:, at].astype(F32) + proj).astype(BF)
        out.wait()

    vmem = pl.BlockSpec(memory_space=pltpu.VMEM)
    hbm = pl.BlockSpec(memory_space=pl.ANY)
    return pl.pallas_call(
        kernel,
        out_shape=(
            jax.ShapeDtypeStruct((rows, width), BF),
            jax.ShapeDtypeStruct((width, width), BF),
        ),
        in_specs=[pl.BlockSpec(memory_space=pltpu.SMEM), vmem, vmem] + [hbm] * count,
        out_specs=(vmem, hbm),
        scratch_shapes=[
            pltpu.VMEM((width, width), BF),
            pltpu.SemaphoreType.DMA((count,)),
            pltpu.SemaphoreType.DMA,
        ],
        compiler_params=pltpu.CompilerParams(vmem_limit_bytes=VMEM_BYTES),
        cost_estimate=pl.CostEstimate(
            flops=2 * rows * width * width, bytes_accessed=4 * width * width, transcendentals=0
        ),
        name="project",
    )(places, gated, frames, *pieces)


def line_scatter(term, kind):
    count = lax.axis_size("seq")
    here = lax.axis_index("seq")

    def block(index):
        index = jnp.clip(index, 0, count - 1)
        return lax.dynamic_index_in_dim(term, index, 0, keepdims=False).astype(F32)

    up = down = None
    for step in range(1, count):
        to_up = block(here + count - step)
        to_down = block(here - count + step)
        if up is not None:
            to_up = to_up + up.astype(F32)
            to_down = to_down + down.astype(F32)
        up = lax.ppermute(to_up.astype(kind), "seq", [(i, i + 1) for i in range(step)])
        down = lax.ppermute(
            to_down.astype(kind), "seq", [(i, i - 1) for i in range(count - step, count)]
        )
    return block(here) + up.astype(F32) + down.astype(F32)


def halo_edges(first, last):
    count = lax.axis_size("seq")
    forward = [(i, i + 1) for i in range(count - 1)]
    backward = [(i + 1, i) for i in range(count - 1)]
    return lax.ppermute(last, "seq", forward), lax.ppermute(first, "seq", backward)


EDGE = 16
LOGIT_TILE = 512
LANES = 128


def channel_tile(width):
    return 256 if width % 256 == 0 else width


def fill(pad_ref, low_ref, mid_ref, high_ref):
    rows = mid_ref.shape[0]
    pad_ref[:EDGE, :] = low_ref[...].astype(F32)
    pad_ref[EDGE : EDGE + rows, :] = mid_ref[...].astype(F32)
    pad_ref[EDGE + rows :, :] = high_ref[...].astype(F32)


def tap_specs(rows, tile):
    edge = pl.BlockSpec((EDGE, tile), lambda j: (0, j))
    return edge, pl.BlockSpec((rows, tile), lambda j: (0, j))


def convolve(low, frames, high, taps):
    rows, width = frames.shape
    count = taps.shape[0]
    first = EDGE - (count - 1) // 2
    tile = channel_tile(width)

    def kernel(
        low_ref, mid_ref, high_ref, taps_ref, conv_ref, gated_ref, turned_ref, mark_ref, pad_ref
    ):
        mark_ref[...] = jnp.zeros_like(mark_ref)
        fill(pad_ref, low_ref, mid_ref, high_ref)
        for lane in range(0, tile, LANES):
            at = slice(lane, lane + LANES)
            conv = jnp.zeros((rows, LANES), F32)
            for k in range(count):
                conv = conv + taps_ref[k : k + 1, at] * pad_ref[first + k : first + k + rows, at]
            conv_ref[:, at] = conv
            gated = conv / (1.0 + jnp.exp(-conv))
            gated_ref[:, at] = gated.astype(BF)
            turned_ref[at, :] = gated.T.astype(BF)

    edge, body_spec = tap_specs(rows, tile)
    return pl.pallas_call(
        kernel,
        grid=(width // tile,),
        out_shape=(
            jax.ShapeDtypeStruct((rows, width), F32),
            jax.ShapeDtypeStruct((rows, width), BF),
            jax.ShapeDtypeStruct((width, rows), BF),
            jax.ShapeDtypeStruct((8, LANES), F32),
        ),
        in_specs=[edge, body_spec, edge, pl.BlockSpec((count, tile), lambda j: (0, j))],
        out_specs=(
            body_spec,
            body_spec,
            pl.BlockSpec((tile, rows), lambda j: (j, 0)),
            pl.BlockSpec((8, LANES), lambda j: (0, 0)),
        ),
        scratch_shapes=[pltpu.VMEM((rows + 2 * EDGE, tile), F32)],
        compiler_params=pltpu.CompilerParams(vmem_limit_bytes=VMEM_BYTES),
        cost_estimate=CHEAP,
        name="convolve",
    )(low, frames, high, taps)


def convolve_back(low, dconv, high, taps, dmixed):
    rows, width = dconv.shape
    count = taps.shape[0]
    last = EDGE + (count - 1) // 2
    tile = channel_tile(width)

    def kernel(low_ref, mid_ref, high_ref, taps_ref, dmixed_ref, out_ref, pad_ref):
        fill(pad_ref, low_ref, mid_ref, high_ref)
        for lane in range(0, tile, LANES):
            at = slice(lane, lane + LANES)
            back = dmixed_ref[:, at].astype(F32)
            for k in range(count):
                back = back + taps_ref[k : k + 1, at] * pad_ref[last - k : last - k + rows, at]
            out_ref[:, at] = back.astype(BF)

    edge, body_spec = tap_specs(rows, tile)
    return pl.pallas_call(
        kernel,
        grid=(width // tile,),
        out_shape=jax.ShapeDtypeStruct((rows, width), BF),
        in_specs=[edge, body_spec, edge, pl.BlockSpec((count, tile), lambda j: (0, j)), body_spec],
        out_specs=body_spec,
        scratch_shapes=[pltpu.VMEM((rows + 2 * EDGE, tile), F32)],
        compiler_params=pltpu.CompilerParams(vmem_limit_bytes=VMEM_BYTES),
        cost_estimate=CHEAP,
        name="convolve_back",
    )(low, dconv, high, taps, dmixed)


def gate_back(dmixed, pw_full, conv, low, frames, high, count, earlier):
    rows, width = dmixed.shape
    first = EDGE - (count - 1) // 2
    tile = channel_tile(width)
    held = -(-count // 16) * 16

    def kernel(
        dmixed_ref, pw_ref, conv_ref, low_ref, mid_ref, high_ref, _, dconv_ref, taps_ref, pad_ref
    ):
        fill(pad_ref, low_ref, mid_ref, high_ref)
        dgated = lax.dot_general(
            dmixed_ref[...], pw_ref[...], (((1,), (1,)), ((), ())), preferred_element_type=F32
        )
        conv = conv_ref[...]
        sig = 1.0 / (1.0 + jnp.exp(-conv))
        dconv_ref[...] = (dgated * sig * (1.0 + conv * (1.0 - sig))).astype(BF)
        taps_ref[...] = jnp.zeros_like(taps_ref)
        for lane in range(0, tile, LANES):
            at = slice(lane, lane + LANES)
            dconv = dconv_ref[:, at].astype(F32)
            for k in range(count):
                term = dconv * pad_ref[first + k : first + k + rows, at]
                taps_ref[k : k + 1, at] = jnp.sum(term, axis=0, keepdims=True)

    edge, body_spec = tap_specs(rows, tile)
    return pl.pallas_call(
        kernel,
        grid=(width // tile,),
        out_shape=(
            jax.ShapeDtypeStruct((rows, width), BF),
            jax.ShapeDtypeStruct((held, width), F32),
        ),
        in_specs=[
            pl.BlockSpec((rows, width), lambda j: (0, 0)),
            pl.BlockSpec((tile, width), lambda j: (j, 0)),
            body_spec,
            edge,
            body_spec,
            edge,
            pl.BlockSpec(memory_space=pl.ANY),
        ],
        out_specs=(body_spec, pl.BlockSpec((held, tile), lambda j: (0, j))),
        scratch_shapes=[pltpu.VMEM((rows + 2 * EDGE, tile), F32)],
        compiler_params=pltpu.CompilerParams(vmem_limit_bytes=VMEM_BYTES),
        cost_estimate=pl.CostEstimate(
            flops=6 * 10**9, bytes_accessed=44 * 10**6, transcendentals=0
        ),
        name="gate_back",
    )(dmixed, pw_full, conv, low, frames, high, earlier)


def head_terms(left_own, left_other, right_own, right_other, earlier):
    width = left_own[0].shape[1]
    depth, vocab = right_own.shape
    split = left_own[0].shape[0]
    tile = channel_tile(width)

    def kernel(near_a, far_a, near_b, far_b, ra_ref, rb_ref, _, out_ref):
        lhs = (((0,), (0,)), ((), ()))
        term = jnp.zeros(out_ref.shape, F32)
        for near, far, right in ((near_a, far_a, ra_ref), (near_b, far_b, rb_ref)):
            term += lax.dot_general(near[...], right[:split], lhs, preferred_element_type=F32)
            term += lax.dot_general(far[...], right[split:], lhs, preferred_element_type=F32)
        out_ref[...] = term.astype(BF)

    near = pl.BlockSpec((split, tile), lambda j: (0, j))
    far = pl.BlockSpec((depth - split, tile), lambda j: (0, j))
    right = pl.BlockSpec((depth, vocab), lambda j: (0, 0))
    return pl.pallas_call(
        kernel,
        grid=(width // tile,),
        out_shape=jax.ShapeDtypeStruct((width, vocab), BF),
        in_specs=[near, far, near, far, right, right, pl.BlockSpec(memory_space=pl.ANY)],
        out_specs=pl.BlockSpec((tile, vocab), lambda j: (j, 0)),
        compiler_params=pltpu.CompilerParams(vmem_limit_bytes=VMEM_BYTES),
        cost_estimate=pl.CostEstimate(
            flops=13 * 10**9, bytes_accessed=40 * 10**6, transcendentals=0
        ),
        name="head_terms",
    )(*left_own, *left_other, right_own, right_other, earlier)


def logits_and_stats(mixed, head, other):
    rows, width = mixed.shape
    vocab = head.shape[1]
    tile = min(LOGIT_TILE, vocab)
    steps = vocab // tile

    def kernel(x_ref, a_ref, b_ref, la_ref, lb_ref, stats_ref, top_ref, total_ref):
        step = pl.program_id(0)

        @pl.when(step == 0)
        def _():
            top_ref[...] = jnp.full_like(top_ref, -jnp.inf)
            total_ref[...] = jnp.zeros_like(total_ref)

        la_ref[...] = jnp.dot(x_ref[...], a_ref[...], preferred_element_type=F32)
        lb_ref[...] = jnp.dot(x_ref[...], b_ref[...], preferred_element_type=F32)
        parts = [
            ref[:, lane : lane + LANES] for ref in (la_ref, lb_ref) for lane in range(0, tile, LANES)
        ]
        old = top_ref[...]
        new = old
        for part in parts:
            new = jnp.maximum(new, part)
        total = total_ref[...] * jnp.exp(old - new)
        for part in parts:
            total = total + jnp.exp(part - new)
        top_ref[...] = new
        total_ref[...] = total

        @pl.when(step == steps - 1)
        def _():
            tops, totals = new.T, total.T
            top = jnp.max(tops, axis=0, keepdims=True)
            total_row = jnp.sum(totals * jnp.exp(tops - top), axis=0, keepdims=True)
            row = lax.broadcasted_iota(jnp.int32, (8, rows), 0)
            stats_ref[...] = jnp.where(row == 0, top, total_row)

    columns = pl.BlockSpec((width, tile), lambda j: (0, j))
    made = pl.BlockSpec((rows, tile), lambda j: (0, j))
    return pl.pallas_call(
        kernel,
        grid=(steps,),
        out_shape=(
            jax.ShapeDtypeStruct((rows, vocab), F32),
            jax.ShapeDtypeStruct((rows, vocab), F32),
            jax.ShapeDtypeStruct((8, rows), F32),
        ),
        in_specs=[pl.BlockSpec((rows, width), lambda j: (0, 0)), columns, columns],
        out_specs=(made, made, pl.BlockSpec((8, rows), lambda j: (0, 0))),
        scratch_shapes=[pltpu.VMEM((rows, 128), F32), pltpu.VMEM((rows, 128), F32)],
        compiler_params=pltpu.CompilerParams(vmem_limit_bytes=VMEM_BYTES),
        cost_estimate=pl.CostEstimate(flops=0, bytes_accessed=0, transcendentals=0),
        name="logits",
    )(mixed, head, other)


def logit_gradients(firsts, near, far, stats, labels):
    chips = len(stats)
    rows, vocab = far[0].shape
    tile = min(LOGIT_TILE, vocab)

    def kernel(*refs):
        first_ref = refs[0]
        logit_refs = [refs[1 + 2 * m : 3 + 2 * m] for m in range(chips)]
        stat_refs = refs[1 + 2 * chips : 1 + 3 * chips]
        label_refs = refs[1 + 3 * chips : 1 + 4 * chips]
        own_ref, other_ref, columns_ref = refs[1 + 4 * chips :]
        step = pl.program_id(0)

        @pl.when(step == 0)
        def _():
            for m in range(chips):
                tops, totals = [], []
                for o in range(chips):
                    at = m ^ o
                    tops.append(stat_refs[o][at : at + 1, :])
                    totals.append(stat_refs[o][chips + at : chips + at + 1, :])
                top = tops[0]
                for t in tops[1:]:
                    top = jnp.maximum(top, t)
                total = sum(s * jnp.exp(t - top) for s, t in zip(totals, tops))
                values = jnp.concatenate(
                    [
                        top,
                        1.0 / total,
                        label_refs[m][0:1, :],
                        label_refs[m][1:2, :],
                        jnp.zeros((124, rows), F32),
                    ],
                    axis=0,
                )
                columns_ref[m] = values.T

        entries = lax.broadcasted_iota(jnp.int32, (rows, tile), 1) + step * tile
        for m in range(chips):
            columns = columns_ref[m]
            top, inverse = columns[:, 0:1], columns[:, 1:2]
            target = columns[:, 2:3].astype(jnp.int32)
            weight = columns[:, 3:4]
            for k, out_ref in enumerate((own_ref, other_ref)):
                probs = jnp.exp(logit_refs[m][k][...] - top) * inverse
                hit = (entries == target - first_ref[k]).astype(F32)
                out_ref[m * rows : (m + 1) * rows, :] = (weight * (probs - hit)).astype(BF)

    def block(index):
        return pl.BlockSpec((rows, tile), lambda j: (index, j))

    made = pl.BlockSpec((chips * rows, tile), lambda j: (0, j))
    return pl.pallas_call(
        kernel,
        grid=(vocab // tile,),
        out_shape=(
            jax.ShapeDtypeStruct((chips * rows, vocab), BF),
            jax.ShapeDtypeStruct((chips * rows, vocab), BF),
        ),
        in_specs=[pl.BlockSpec(memory_space=pltpu.SMEM)]
        + [block(m) for m in range(chips - 1) for _ in range(2)]
        + [block(0)] * 2
        + [pl.BlockSpec((2 * chips, rows), lambda j: (0, 0))] * chips
        + [pl.BlockSpec((2, rows), lambda j: (0, 0))] * chips,
        out_specs=(made, made),
        scratch_shapes=[pltpu.VMEM((chips, rows, 128), F32)],
        compiler_params=pltpu.CompilerParams(vmem_limit_bytes=VMEM_BYTES),
        cost_estimate=pl.CostEstimate(flops=0, bytes_accessed=0, transcendentals=0),
        name="dlogits",
    )(firsts, *(list(near) * (chips - 1)), *far, *stats, *labels)


def body(frames, conv_kernel, pw_weight, head_weight, targets, frame_weight):
    frames = frames[0]
    rows, width = frames.shape
    taps = conv_kernel.shape[0]
    seqs = lax.axis_size("seq")
    count = lax.axis_size("fsdp")
    chips = count // 2
    me = lax.axis_index("fsdp")
    chip = me // 2
    core = me % 2
    low, high = halo_edges(frames[:EDGE], frames[-EDGE:])
    conv, gated, turned, mark = convolve(low, frames, high, conv_kernel)
    shard = pw_weight.shape[0]
    pieces, places = [], []
    gathered = gather_pieces(pw_weight, mark)
    for piece, m, first in gathered:
        pieces += [piece, swap(piece, 1)]
        places += [(me ^ (2 * m)) * shard + first, (me ^ (2 * m + 1)) * shard + first]
    places = jnp.stack(places).astype(jnp.int32)
    head_other = swap(head_weight, 1)

    mixed, pw_full = project(gated, frames, pieces, places)
    labels = jnp.stack([targets[0].astype(F32), frame_weight[0].astype(F32)])
    all_labels = [labels] + [swap(labels, 2 * m) for m in range(1, chips)]

    piece = width // (seqs * count)
    gated_t = turned.reshape(seqs, chips, 2, piece, rows)
    gated_t = jnp.stack(
        [lax.dynamic_index_in_dim(gated_t, chip ^ m, 1, keepdims=False) for m in range(chips)]
    )
    gated_own = lax.dynamic_index_in_dim(gated_t, core, 2, keepdims=False)
    gated_sent = lax.dynamic_index_in_dim(gated_t, 1 - core, 2, keepdims=False)
    gated_got = swap(gated_sent, 1)
    gated_pair = jnp.concatenate([gated_own, gated_got], axis=-1)

    weights = (head_weight, head_other)
    vocab = head_weight.shape[1]
    pairs, tops, totals = [], [], []

    def near_logits(block):
        own, other, stats = logits_and_stats(block, *weights)
        pairs.append((own, other))
        tops.append(stats[0].reshape(-1, rows))
        totals.append(stats[1].reshape(-1, rows))
        return (stats,)

    near_own, far_own = gather_rows(mixed, (gated_got,), near_logits)
    pair = [jnp.dot(far_own, w, preferred_element_type=F32) for w in weights]
    top = jnp.maximum(jnp.max(pair[0], axis=1), jnp.max(pair[1], axis=1))
    total = sum(jnp.sum(jnp.exp(l - top[:, None]), axis=1) for l in pair)
    pairs.append(pair)
    tops.append(top.reshape(-1, rows))
    totals.append(total.reshape(-1, rows))
    near_other = swap(near_own, 1)
    far_other = swap(far_own, 1)
    packed = jnp.concatenate(tops + totals)
    got = [packed] + [swap(packed, 2 * m) for m in range(1, chips)]
    firsts = jnp.stack([me * vocab, (me ^ 1) * vocab]).astype(jnp.int32)
    right_own, right_sent = logit_gradients(firsts, pairs[0], pairs[1], got, all_labels)
    right_other = swap(right_sent, 1)

    def back_head(m):
        rhs = (((1,), (1,)), ((), ()))
        at = slice(m * rows, (m + 1) * rows)
        return lax.dot_general(
            right_own[at], head_weight, rhs, preferred_element_type=F32
        ) + lax.dot_general(right_sent[at], head_other, rhs, preferred_element_type=F32)

    terms = []

    def while_dmixed_travels(_, sent):
        terms.append(
            head_terms((near_own, far_own), (near_other, far_other), right_own, right_other, sent)
        )
        return (), (terms[0],)

    dmixed, _, _ = scatter_and_finish(
        back_head, lambda m: (back_head(m), 0), chips, (), while_dmixed_travels, BF
    )
    head_grad = lax.psum_scatter(terms[0], "seq", scatter_dimension=0, tiled=True).astype(F32)

    dmixed_pair = jnp.concatenate([dmixed, swap(dmixed, 1)], axis=0)
    pw_term = jnp.dot(
        gated_pair.reshape(-1, 2 * rows), dmixed_pair, preferred_element_type=F32
    )
    dconv, kernel_rows = gate_back(
        dmixed, pw_full, conv, low, frames, high, taps, pw_term[:8, :LANES]
    )
    size = seqs * piece
    first = core == 0
    share = kernel_rows.shape[0] // 2

    def while_pw_travels(kept, _):
        dlow, dhigh = halo_edges(*kept[:2])
        low_taps, high_taps = kept[2][:share], kept[2][share:]
        part = jnp.where(first, low_taps, high_taps) + swap(
            jnp.where(first, high_taps, low_taps), 1
        )
        terms = [part] + [
            lax.ppermute(part, "seq", [(i, i ^ m) for i in range(seqs)]) for m in range(1, seqs)
        ]
        while len(terms) > 1:
            terms = [terms[n] + terms[n + 1] for n in range(0, len(terms), 2)]
        total = terms[0]
        backs.append(convolve_back(dlow, dconv, dhigh, conv_kernel, dmixed))
        return (total,), (backs[0],)

    backs = []
    pw_sum, _, (kernel_sum,) = scatter_and_finish(
        lambda m: pw_term[m * size : (m + 1) * size],
        lambda m: (pw_term, m),
        chips,
        (
            (dconv, EDGE, 0),
            (dconv, EDGE, rows // EDGE - 1),
            (kernel_rows, kernel_rows.shape[0], 0),
        ),
        while_pw_travels,
        F32,
    )
    back = backs[0]
    pw_sum = pw_sum.reshape(seqs, piece, width)
    here = lax.axis_index("seq")

    def shard_of(m):
        return lax.dynamic_index_in_dim(pw_sum, here ^ m, 0, keepdims=False)

    pw_grad = shard_of(0)
    for m in range(1, seqs):
        moved = lax.ppermute(
            shard_of(m).astype(BF), "seq", [(i, i ^ m) for i in range(seqs)]
        )
        pw_grad = pw_grad + moved.astype(F32)

    mask = 2
    while mask < count:
        kernel_sum = kernel_sum + swap(kernel_sum, mask)
        mask *= 2
    kernel_got = swap(kernel_sum, 1)
    kernel_grad = jnp.concatenate(
        [
            jnp.where(first, kernel_sum, kernel_got),
            jnp.where(first, kernel_got, kernel_sum)[: taps - share],
        ],
        axis=0,
    )
    return (back[None], kernel_grad, pw_grad, head_grad)


def solution(mesh):
    return jax.shard_map(
        body,
        mesh=mesh,
        in_specs=(
            P("fsdp", "seq", None),
            P(),
            P("fsdp", None),
            P(None, "fsdp"),
            P("fsdp", "seq"),
            P("fsdp", "seq"),
        ),
        out_specs=(P("fsdp", "seq", None), P(), P(("seq", "fsdp"), None), P("seq", "fsdp")),
        check_vma=False,
    )
```

```python
import jax
import jax.numpy as jnp
from jax import lax
from jax.experimental import pallas as pl
from jax.experimental.pallas import tpu as pltpu
from jax.sharding import PartitionSpec as P

BF = jnp.bfloat16
F32 = jnp.float32


def swap(value, mask):
    count = lax.axis_size("fsdp")
    return lax.ppermute(value, "fsdp", [(i, i ^ mask) for i in range(count)])


VMEM_BYTES = 56 * 2**20
CHEAP = pl.CostEstimate(flops=0, bytes_accessed=0, transcendentals=0)


def halves_to_forward(from_x, from_y, *earlier):
    rows, width = from_x.shape
    half = rows // 2

    def kernel(x_ref, y_ref, *refs):
        low_ref, high_ref = refs[len(earlier) :]
        low_ref[...] = x_ref[...]
        high_ref[...] = y_ref[...]

    made = jax.ShapeDtypeStruct((half, width), from_x.dtype)
    whole = pl.BlockSpec((half, width), lambda j: (0, 0))
    return pl.pallas_call(
        kernel,
        grid=(1,),
        out_shape=(made, made),
        in_specs=[
            pl.BlockSpec((half, width), lambda j: (0, 0)),
            pl.BlockSpec((half, width), lambda j: (1, 0)),
        ]
        + [pl.BlockSpec(memory_space=pl.ANY)] * len(earlier),
        out_specs=(whole, whole),
        compiler_params=pltpu.CompilerParams(vmem_limit_bytes=VMEM_BYTES),
        cost_estimate=CHEAP,
        name="forward",
    )(from_x, from_y, *earlier)


def near_and_forward(block, from_x, from_y, *earlier):
    rows, width = block.shape
    half = rows // 2

    def kernel(own_ref, x_ref, y_ref, *refs):
        near_ref, low_ref, high_ref = refs[len(earlier) :]
        near_ref[:rows, :] = own_ref[...]
        near_ref[rows : 2 * rows, :] = x_ref[...]
        near_ref[2 * rows :, :] = y_ref[...]
        low_ref[...] = x_ref[:half, :]
        high_ref[...] = y_ref[half:, :]

    def spec(count):
        return pl.BlockSpec((count, width), lambda j: (0, 0))

    made = jax.ShapeDtypeStruct((half, width), block.dtype)
    return pl.pallas_call(
        kernel,
        grid=(1,),
        out_shape=(jax.ShapeDtypeStruct((3 * rows, width), block.dtype), made, made),
        in_specs=[spec(rows)] * 3 + [pl.BlockSpec(memory_space=pl.ANY)] * len(earlier),
        out_specs=(spec(3 * rows), spec(half), spec(half)),
        compiler_params=pltpu.CompilerParams(vmem_limit_bytes=VMEM_BYTES),
        cost_estimate=CHEAP,
        name="near_and_forward",
    )(block, from_x, from_y, *earlier)


def stack_halves(low, high, *earlier):
    half, width = low.shape

    def kernel(low_ref, high_ref, *refs):
        refs[-1][:half, :] = low_ref[...]
        refs[-1][half:, :] = high_ref[...]

    part = pl.BlockSpec((half, width), lambda j: (0, 0))
    return pl.pallas_call(
        kernel,
        grid=(1,),
        out_shape=jax.ShapeDtypeStruct((2 * half, width), low.dtype),
        in_specs=[part, part] + [pl.BlockSpec(memory_space=pl.ANY)] * len(earlier),
        out_specs=pl.BlockSpec((2 * half, width), lambda j: (0, 0)),
        compiler_params=pltpu.CompilerParams(vmem_limit_bytes=VMEM_BYTES),
        cost_estimate=CHEAP,
        name="stack_halves",
    )(low, high, *earlier)


def gather_rows(block, earlier, between):
    chips = lax.axis_size("fsdp") // 2
    if chips != 4:
        near = jnp.concatenate([block] + [swap(block, 2 * m) for m in range(1, chips - 1)])
        between(near)
        return near, swap(block, 2 * (chips - 1))
    near, to_y, to_x = near_and_forward(block, swap(block, 2), swap(block, 4), *earlier)
    low = swap(to_y, 4)
    high = swap(to_x, 2)
    return near, stack_halves(low, high, *between(near))


def join_halves(near_y, near_x, low, high, earlier, passed=()):
    half, width = low.shape
    rows = 2 * half
    tile = width
    count = len(passed)

    def kernel(y_ref, x_ref, low_ref, high_ref, *refs):
        to_y_ref, to_x_ref = refs[len(earlier) + count : len(earlier) + count + 2]
        to_y_ref[:half, :] = (y_ref[:half, :] + low_ref[...].astype(F32)).astype(BF)
        to_y_ref[half:, :] = y_ref[half:, :].astype(BF)
        to_x_ref[:half, :] = x_ref[:half, :].astype(BF)
        to_x_ref[half:, :] = (x_ref[half:, :] + high_ref[...].astype(F32)).astype(BF)
        for n in range(count):
            refs[len(earlier) + count + 2 + n][...] = refs[n][...]

    def block(size, index):
        return pl.BlockSpec((size, tile), lambda j: (index, j))

    made = jax.ShapeDtypeStruct((rows, width), BF)
    return pl.pallas_call(
        kernel,
        grid=(width // tile,),
        out_shape=(made, made)
        + tuple(jax.ShapeDtypeStruct((size, width), value.dtype) for value, size, _ in passed),
        in_specs=[block(rows, near_y[1]), block(rows, near_x[1]), block(half, 0), block(half, 0)]
        + [block(size, index) for _, size, index in passed]
        + [pl.BlockSpec(memory_space=pl.ANY)] * len(earlier),
        out_specs=(block(rows, 0), block(rows, 0)) + tuple(block(size, 0) for _, size, _ in passed),
        compiler_params=pltpu.CompilerParams(vmem_limit_bytes=VMEM_BYTES),
        cost_estimate=CHEAP,
        name="join_halves",
    )(near_y[0], near_x[0], low, high, *[value for value, _, _ in passed], *earlier)


def gather_pieces(block, *earlier):
    chips = lax.axis_size("fsdp") // 2
    if chips != 4:
        return [(block, 0, 0)] + [(swap(block, 2 * m), m, 0) for m in range(1, chips)]
    half = block.shape[0] // 2
    from_x = swap(block, 2)
    from_y = swap(block, 4)
    if earlier:
        to_y, to_x = halves_to_forward(from_x, from_y, *earlier)
    else:
        to_y, to_x = from_x[:half], from_y[half:]
    far_low = swap(to_y, 4)
    far_high = swap(to_x, 2)
    return [(block, 0, 0), (from_x, 1, 0), (from_y, 2, 0), (far_low, 3, 0), (far_high, 3, half)]


def finish_sum(own, recv_x, recv_y, index, passed, dtype, *earlier):
    rows, width = recv_x.shape
    tile = width
    count = len(passed)

    def kernel(own_ref, x_ref, y_ref, *refs):
        outs = refs[count + len(earlier) :]
        total = own_ref[...] + x_ref[...].astype(F32) + y_ref[...].astype(F32)
        outs[0][...] = total.astype(dtype)
        for n in range(count):
            outs[1 + n][...] = refs[n][...]

    def block(size, at):
        return pl.BlockSpec((size, tile), lambda j: (at, j))

    return pl.pallas_call(
        kernel,
        grid=(width // tile,),
        out_shape=(jax.ShapeDtypeStruct((rows, width), dtype),)
        + tuple(jax.ShapeDtypeStruct(v.shape, v.dtype) for v in passed),
        in_specs=[block(rows, index), block(rows, 0), block(rows, 0)]
        + [block(v.shape[0], 0) for v in passed]
        + [pl.BlockSpec(memory_space=pl.ANY)] * len(earlier),
        out_specs=(block(rows, 0),) + tuple(block(v.shape[0], 0) for v in passed),
        compiler_params=pltpu.CompilerParams(vmem_limit_bytes=VMEM_BYTES),
        cost_estimate=CHEAP,
        name="finish_sum",
    )(own, recv_x, recv_y, *passed, *earlier)


def scatter_and_finish(part, near, chips, passed, last, dtype):
    if chips != 4:
        total = part(0)
        for m in range(1, chips):
            total = total + swap(part(m).astype(BF), 2 * m).astype(F32)
        kept = [v[size * index : size * (index + 1)] for v, size, index in passed]
        return total.astype(dtype), kept, last(kept, total)[0]
    far = part(3).astype(BF)
    half = far.shape[0] // 2
    low = swap(far[:half], 2)
    high = swap(far[half:], 4)
    own, index = near(0)
    to_y, to_x, *kept = join_halves(near(2), near(1), low, high, (own,), passed)
    recv_x, recv_y = swap(to_x, 2), swap(to_y, 4)
    handed, waited = last(kept, to_x)
    total, *handed = finish_sum(own, recv_x, recv_y, index, handed, dtype, *waited)
    return total, kept, handed


def project(gated, frames, pieces, places):
    rows, width = gated.shape
    count = len(pieces)
    tile = 512

    def kernel(*refs):
        place = refs[0]
        gated_ref, frames_ref = refs[1:3]
        piece_refs = refs[3 : 3 + count]
        mixed_ref, full_ref, held, sems, out_sem = refs[3 + count :]
        copies = []
        for n in range(count):
            size = piece_refs[n].shape[0]
            start = pl.multiple_of(place[n], 16)
            copy = pltpu.make_async_copy(piece_refs[n], held.at[pl.ds(start, size)], sems.at[n])
            copy.start()
            copies.append(copy)
        for copy in copies:
            copy.wait()
        out = pltpu.make_async_copy(held, full_ref, out_sem)
        out.start()
        for col in range(0, width, tile):
            at = slice(col, col + tile)
            proj = jnp.dot(gated_ref[...], held[:, at], preferred_element_type=F32)
            mixed_ref[:, at] = (frames_ref[:, at].astype(F32) + proj).astype(BF)
        out.wait()

    vmem = pl.BlockSpec(memory_space=pltpu.VMEM)
    hbm = pl.BlockSpec(memory_space=pl.ANY)
    return pl.pallas_call(
        kernel,
        out_shape=(
            jax.ShapeDtypeStruct((rows, width), BF),
            jax.ShapeDtypeStruct((width, width), BF),
        ),
        in_specs=[pl.BlockSpec(memory_space=pltpu.SMEM), vmem, vmem] + [hbm] * count,
        out_specs=(vmem, hbm),
        scratch_shapes=[
            pltpu.VMEM((width, width), BF),
            pltpu.SemaphoreType.DMA((count,)),
            pltpu.SemaphoreType.DMA,
        ],
        compiler_params=pltpu.CompilerParams(vmem_limit_bytes=VMEM_BYTES),
        cost_estimate=pl.CostEstimate(
            flops=2 * rows * width * width, bytes_accessed=4 * width * width, transcendentals=0
        ),
        name="project",
    )(places, gated, frames, *pieces)


def line_scatter(term, kind):
    count = lax.axis_size("seq")
    here = lax.axis_index("seq")

    def block(index):
        index = jnp.clip(index, 0, count - 1)
        return lax.dynamic_index_in_dim(term, index, 0, keepdims=False).astype(F32)

    up = down = None
    for step in range(1, count):
        to_up = block(here + count - step)
        to_down = block(here - count + step)
        if up is not None:
            to_up = to_up + up.astype(F32)
            to_down = to_down + down.astype(F32)
        up = lax.ppermute(to_up.astype(kind), "seq", [(i, i + 1) for i in range(step)])
        down = lax.ppermute(
            to_down.astype(kind), "seq", [(i, i - 1) for i in range(count - step, count)]
        )
    return block(here) + up.astype(F32) + down.astype(F32)


def halo_edges(first, last):
    count = lax.axis_size("seq")
    forward = [(i, i + 1) for i in range(count - 1)]
    backward = [(i + 1, i) for i in range(count - 1)]
    return lax.ppermute(last, "seq", forward), lax.ppermute(first, "seq", backward)


EDGE = 16
LOGIT_TILE = 512
LANES = 128


def channel_tile(width):
    return 256 if width % 256 == 0 else width


def fill(pad_ref, low_ref, mid_ref, high_ref):
    rows = mid_ref.shape[0]
    pad_ref[:EDGE, :] = low_ref[...].astype(F32)
    pad_ref[EDGE : EDGE + rows, :] = mid_ref[...].astype(F32)
    pad_ref[EDGE + rows :, :] = high_ref[...].astype(F32)


def tap_specs(rows, tile):
    edge = pl.BlockSpec((EDGE, tile), lambda j: (0, j))
    return edge, pl.BlockSpec((rows, tile), lambda j: (0, j))


def convolve(low, frames, high, taps):
    rows, width = frames.shape
    count = taps.shape[0]
    first = EDGE - (count - 1) // 2
    tile = channel_tile(width)

    def kernel(
        low_ref, mid_ref, high_ref, taps_ref, conv_ref, gated_ref, turned_ref, mark_ref, pad_ref
    ):
        mark_ref[...] = jnp.zeros_like(mark_ref)
        fill(pad_ref, low_ref, mid_ref, high_ref)
        for lane in range(0, tile, LANES):
            at = slice(lane, lane + LANES)
            conv = jnp.zeros((rows, LANES), F32)
            for k in range(count):
                conv = conv + taps_ref[k : k + 1, at] * pad_ref[first + k : first + k + rows, at]
            conv_ref[:, at] = conv
            gated = conv / (1.0 + jnp.exp(-conv))
            gated_ref[:, at] = gated.astype(BF)
            turned_ref[at, :] = gated.T.astype(BF)

    edge, body_spec = tap_specs(rows, tile)
    return pl.pallas_call(
        kernel,
        grid=(width // tile,),
        out_shape=(
            jax.ShapeDtypeStruct((rows, width), F32),
            jax.ShapeDtypeStruct((rows, width), BF),
            jax.ShapeDtypeStruct((width, rows), BF),
            jax.ShapeDtypeStruct((8, LANES), F32),
        ),
        in_specs=[edge, body_spec, edge, pl.BlockSpec((count, tile), lambda j: (0, j))],
        out_specs=(
            body_spec,
            body_spec,
            pl.BlockSpec((tile, rows), lambda j: (j, 0)),
            pl.BlockSpec((8, LANES), lambda j: (0, 0)),
        ),
        scratch_shapes=[pltpu.VMEM((rows + 2 * EDGE, tile), F32)],
        compiler_params=pltpu.CompilerParams(vmem_limit_bytes=VMEM_BYTES),
        cost_estimate=CHEAP,
        name="convolve",
    )(low, frames, high, taps)


def convolve_back(low, dconv, high, taps, dmixed):
    rows, width = dconv.shape
    count = taps.shape[0]
    last = EDGE + (count - 1) // 2
    tile = channel_tile(width)

    def kernel(low_ref, mid_ref, high_ref, taps_ref, dmixed_ref, out_ref, pad_ref):
        fill(pad_ref, low_ref, mid_ref, high_ref)
        for lane in range(0, tile, LANES):
            at = slice(lane, lane + LANES)
            back = dmixed_ref[:, at].astype(F32)
            for k in range(count):
                back = back + taps_ref[k : k + 1, at] * pad_ref[last - k : last - k + rows, at]
            out_ref[:, at] = back.astype(BF)

    edge, body_spec = tap_specs(rows, tile)
    return pl.pallas_call(
        kernel,
        grid=(width // tile,),
        out_shape=jax.ShapeDtypeStruct((rows, width), BF),
        in_specs=[edge, body_spec, edge, pl.BlockSpec((count, tile), lambda j: (0, j)), body_spec],
        out_specs=body_spec,
        scratch_shapes=[pltpu.VMEM((rows + 2 * EDGE, tile), F32)],
        compiler_params=pltpu.CompilerParams(vmem_limit_bytes=VMEM_BYTES),
        cost_estimate=CHEAP,
        name="convolve_back",
    )(low, dconv, high, taps, dmixed)


def gate_back(dmixed, pw_full, conv, low, frames, high, count, earlier):
    rows, width = dmixed.shape
    first = EDGE - (count - 1) // 2
    tile = channel_tile(width)
    held = -(-count // 16) * 16

    def kernel(
        dmixed_ref, pw_ref, conv_ref, low_ref, mid_ref, high_ref, _, dconv_ref, taps_ref, pad_ref
    ):
        fill(pad_ref, low_ref, mid_ref, high_ref)
        dgated = lax.dot_general(
            dmixed_ref[...], pw_ref[...], (((1,), (1,)), ((), ())), preferred_element_type=F32
        )
        conv = conv_ref[...]
        sig = 1.0 / (1.0 + jnp.exp(-conv))
        dconv_ref[...] = (dgated * sig * (1.0 + conv * (1.0 - sig))).astype(BF)
        taps_ref[...] = jnp.zeros_like(taps_ref)
        for lane in range(0, tile, LANES):
            at = slice(lane, lane + LANES)
            dconv = dconv_ref[:, at].astype(F32)
            for k in range(count):
                term = dconv * pad_ref[first + k : first + k + rows, at]
                taps_ref[k : k + 1, at] = jnp.sum(term, axis=0, keepdims=True)

    edge, body_spec = tap_specs(rows, tile)
    return pl.pallas_call(
        kernel,
        grid=(width // tile,),
        out_shape=(
            jax.ShapeDtypeStruct((rows, width), BF),
            jax.ShapeDtypeStruct((held, width), F32),
        ),
        in_specs=[
            pl.BlockSpec((rows, width), lambda j: (0, 0)),
            pl.BlockSpec((tile, width), lambda j: (j, 0)),
            body_spec,
            edge,
            body_spec,
            edge,
            pl.BlockSpec(memory_space=pl.ANY),
        ],
        out_specs=(body_spec, pl.BlockSpec((held, tile), lambda j: (0, j))),
        scratch_shapes=[pltpu.VMEM((rows + 2 * EDGE, tile), F32)],
        compiler_params=pltpu.CompilerParams(vmem_limit_bytes=VMEM_BYTES),
        cost_estimate=pl.CostEstimate(
            flops=6 * 10**9, bytes_accessed=44 * 10**6, transcendentals=0
        ),
        name="gate_back",
    )(dmixed, pw_full, conv, low, frames, high, earlier)


def head_terms(left_own, left_other, right_own, right_other, earlier):
    width = left_own[0].shape[1]
    depth, vocab = right_own.shape
    split = left_own[0].shape[0]
    tile = channel_tile(width)

    def kernel(near_a, far_a, near_b, far_b, ra_ref, rb_ref, _, out_ref):
        lhs = (((0,), (0,)), ((), ()))
        term = jnp.zeros(out_ref.shape, F32)
        for near, far, right in ((near_a, far_a, ra_ref), (near_b, far_b, rb_ref)):
            term += lax.dot_general(near[...], right[:split], lhs, preferred_element_type=F32)
            term += lax.dot_general(far[...], right[split:], lhs, preferred_element_type=F32)
        out_ref[...] = term.astype(BF)

    near = pl.BlockSpec((split, tile), lambda j: (0, j))
    far = pl.BlockSpec((depth - split, tile), lambda j: (0, j))
    right = pl.BlockSpec((depth, vocab), lambda j: (0, 0))
    return pl.pallas_call(
        kernel,
        grid=(width // tile,),
        out_shape=jax.ShapeDtypeStruct((width, vocab), BF),
        in_specs=[near, far, near, far, right, right, pl.BlockSpec(memory_space=pl.ANY)],
        out_specs=pl.BlockSpec((tile, vocab), lambda j: (j, 0)),
        compiler_params=pltpu.CompilerParams(vmem_limit_bytes=VMEM_BYTES),
        cost_estimate=pl.CostEstimate(
            flops=13 * 10**9, bytes_accessed=40 * 10**6, transcendentals=0
        ),
        name="head_terms",
    )(*left_own, *left_other, right_own, right_other, earlier)


def logits_and_stats(mixed, head, other):
    rows, width = mixed.shape
    vocab = head.shape[1]
    tile = min(LOGIT_TILE, vocab)
    steps = vocab // tile

    def kernel(x_ref, a_ref, b_ref, la_ref, lb_ref, stats_ref, top_ref, total_ref):
        step = pl.program_id(0)

        @pl.when(step == 0)
        def _():
            top_ref[...] = jnp.full_like(top_ref, -jnp.inf)
            total_ref[...] = jnp.zeros_like(total_ref)

        la_ref[...] = jnp.dot(x_ref[...], a_ref[...], preferred_element_type=F32)
        lb_ref[...] = jnp.dot(x_ref[...], b_ref[...], preferred_element_type=F32)
        parts = [
            ref[:, lane : lane + LANES] for ref in (la_ref, lb_ref) for lane in range(0, tile, LANES)
        ]
        old = top_ref[...]
        new = old
        for part in parts:
            new = jnp.maximum(new, part)
        total = total_ref[...] * jnp.exp(old - new)
        for part in parts:
            total = total + jnp.exp(part - new)
        top_ref[...] = new
        total_ref[...] = total

        @pl.when(step == steps - 1)
        def _():
            tops, totals = new.T, total.T
            top = jnp.max(tops, axis=0, keepdims=True)
            total_row = jnp.sum(totals * jnp.exp(tops - top), axis=0, keepdims=True)
            row = lax.broadcasted_iota(jnp.int32, (8, rows), 0)
            stats_ref[...] = jnp.where(row == 0, top, total_row)

    columns = pl.BlockSpec((width, tile), lambda j: (0, j))
    made = pl.BlockSpec((rows, tile), lambda j: (0, j))
    return pl.pallas_call(
        kernel,
        grid=(steps,),
        out_shape=(
            jax.ShapeDtypeStruct((rows, vocab), F32),
            jax.ShapeDtypeStruct((rows, vocab), F32),
            jax.ShapeDtypeStruct((8, rows), F32),
        ),
        in_specs=[pl.BlockSpec((rows, width), lambda j: (0, 0)), columns, columns],
        out_specs=(made, made, pl.BlockSpec((8, rows), lambda j: (0, 0))),
        scratch_shapes=[pltpu.VMEM((rows, 128), F32), pltpu.VMEM((rows, 128), F32)],
        compiler_params=pltpu.CompilerParams(vmem_limit_bytes=VMEM_BYTES),
        cost_estimate=pl.CostEstimate(flops=0, bytes_accessed=0, transcendentals=0),
        name="logits",
    )(mixed, head, other)


def logit_gradients(firsts, near, far, stats, labels):
    chips = len(stats)
    rows, vocab = far[0].shape
    tile = min(LOGIT_TILE, vocab)

    def kernel(*refs):
        first_ref = refs[0]
        logit_refs = [refs[1 + 2 * m : 3 + 2 * m] for m in range(chips)]
        stat_refs = refs[1 + 2 * chips : 1 + 3 * chips]
        label_refs = refs[1 + 3 * chips : 1 + 4 * chips]
        own_ref, other_ref, columns_ref = refs[1 + 4 * chips :]
        step = pl.program_id(0)

        @pl.when(step == 0)
        def _():
            for m in range(chips):
                tops, totals = [], []
                for o in range(chips):
                    at = m ^ o
                    tops.append(stat_refs[o][at : at + 1, :])
                    totals.append(stat_refs[o][chips + at : chips + at + 1, :])
                top = tops[0]
                for t in tops[1:]:
                    top = jnp.maximum(top, t)
                total = sum(s * jnp.exp(t - top) for s, t in zip(totals, tops))
                values = jnp.concatenate(
                    [
                        top,
                        1.0 / total,
                        label_refs[m][0:1, :],
                        label_refs[m][1:2, :],
                        jnp.zeros((124, rows), F32),
                    ],
                    axis=0,
                )
                columns_ref[m] = values.T

        entries = lax.broadcasted_iota(jnp.int32, (rows, tile), 1) + step * tile
        for m in range(chips):
            columns = columns_ref[m]
            top, inverse = columns[:, 0:1], columns[:, 1:2]
            target = columns[:, 2:3].astype(jnp.int32)
            weight = columns[:, 3:4]
            for k, out_ref in enumerate((own_ref, other_ref)):
                probs = jnp.exp(logit_refs[m][k][...] - top) * inverse
                hit = (entries == target - first_ref[k]).astype(F32)
                out_ref[m * rows : (m + 1) * rows, :] = (weight * (probs - hit)).astype(BF)

    def block(index):
        return pl.BlockSpec((rows, tile), lambda j: (index, j))

    made = pl.BlockSpec((chips * rows, tile), lambda j: (0, j))
    return pl.pallas_call(
        kernel,
        grid=(vocab // tile,),
        out_shape=(
            jax.ShapeDtypeStruct((chips * rows, vocab), BF),
            jax.ShapeDtypeStruct((chips * rows, vocab), BF),
        ),
        in_specs=[pl.BlockSpec(memory_space=pltpu.SMEM)]
        + [block(m) for m in range(chips - 1) for _ in range(2)]
        + [block(0)] * 2
        + [pl.BlockSpec((2 * chips, rows), lambda j: (0, 0))] * chips
        + [pl.BlockSpec((2, rows), lambda j: (0, 0))] * chips,
        out_specs=(made, made),
        scratch_shapes=[pltpu.VMEM((chips, rows, 128), F32)],
        compiler_params=pltpu.CompilerParams(vmem_limit_bytes=VMEM_BYTES),
        cost_estimate=pl.CostEstimate(flops=0, bytes_accessed=0, transcendentals=0),
        name="dlogits",
    )(firsts, *(list(near) * (chips - 1)), *far, *stats, *labels)


def body(frames, conv_kernel, pw_weight, head_weight, targets, frame_weight):
    frames = frames[0]
    rows, width = frames.shape
    taps = conv_kernel.shape[0]
    seqs = lax.axis_size("seq")
    count = lax.axis_size("fsdp")
    chips = count // 2
    me = lax.axis_index("fsdp")
    chip = me // 2
    core = me % 2
    low, high = halo_edges(frames[:EDGE], frames[-EDGE:])
    conv, gated, turned, mark = convolve(low, frames, high, conv_kernel)
    shard = pw_weight.shape[0]
    pieces, places = [], []
    gathered = gather_pieces(pw_weight, mark)
    for piece, m, first in gathered:
        pieces += [piece, swap(piece, 1)]
        places += [(me ^ (2 * m)) * shard + first, (me ^ (2 * m + 1)) * shard + first]
    places = jnp.stack(places).astype(jnp.int32)
    head_other = swap(head_weight, 1)

    mixed, pw_full = project(gated, frames, pieces, places)
    labels = jnp.stack([targets[0].astype(F32), frame_weight[0].astype(F32)])
    all_labels = [labels] + [swap(labels, 2 * m) for m in range(1, chips)]

    piece = width // (seqs * count)
    gated_t = turned.reshape(seqs, chips, 2, piece, rows)
    gated_t = jnp.stack(
        [lax.dynamic_index_in_dim(gated_t, chip ^ m, 1, keepdims=False) for m in range(chips)]
    )
    gated_own = lax.dynamic_index_in_dim(gated_t, core, 2, keepdims=False)
    gated_sent = lax.dynamic_index_in_dim(gated_t, 1 - core, 2, keepdims=False)
    gated_got = swap(gated_sent, 1)
    gated_pair = jnp.concatenate([gated_own, gated_got], axis=-1)

    weights = (head_weight, head_other)
    vocab = head_weight.shape[1]
    pairs, tops, totals = [], [], []

    def near_logits(block):
        own, other, stats = logits_and_stats(block, *weights)
        pairs.append((own, other))
        tops.append(stats[0].reshape(-1, rows))
        totals.append(stats[1].reshape(-1, rows))
        return (stats,)

    near_own, far_own = gather_rows(mixed, (gated_got,), near_logits)
    pair = [jnp.dot(far_own, w, preferred_element_type=F32) for w in weights]
    top = jnp.maximum(jnp.max(pair[0], axis=1), jnp.max(pair[1], axis=1))
    total = sum(jnp.sum(jnp.exp(l - top[:, None]), axis=1) for l in pair)
    pairs.append(pair)
    tops.append(top.reshape(-1, rows))
    totals.append(total.reshape(-1, rows))
    near_other = swap(near_own, 1)
    far_other = swap(far_own, 1)
    packed = jnp.concatenate(tops + totals)
    got = [packed] + [swap(packed, 2 * m) for m in range(1, chips)]
    firsts = jnp.stack([me * vocab, (me ^ 1) * vocab]).astype(jnp.int32)
    right_own, right_sent = logit_gradients(firsts, pairs[0], pairs[1], got, all_labels)
    right_other = swap(right_sent, 1)

    def back_head(m):
        rhs = (((1,), (1,)), ((), ()))
        at = slice(m * rows, (m + 1) * rows)
        return lax.dot_general(
            right_own[at], head_weight, rhs, preferred_element_type=F32
        ) + lax.dot_general(right_sent[at], head_other, rhs, preferred_element_type=F32)

    terms = []

    def while_dmixed_travels(_, sent):
        terms.append(
            head_terms((near_own, far_own), (near_other, far_other), right_own, right_other, sent)
        )
        return (), (terms[0],)

    dmixed, _, _ = scatter_and_finish(
        back_head, lambda m: (back_head(m), 0), chips, (), while_dmixed_travels, BF
    )
    head_grad = lax.psum_scatter(terms[0], "seq", scatter_dimension=0, tiled=True).astype(F32)

    dmixed_pair = jnp.concatenate([dmixed, swap(dmixed, 1)], axis=0)
    pw_term = jnp.dot(
        gated_pair.reshape(-1, 2 * rows), dmixed_pair, preferred_element_type=F32
    )
    dconv, kernel_rows = gate_back(
        dmixed, pw_full, conv, low, frames, high, taps, pw_term[:8, :LANES]
    )
    size = seqs * piece
    first = core == 0
    share = kernel_rows.shape[0] // 2

    def while_pw_travels(kept, _):
        dlow, dhigh = halo_edges(*kept[:2])
        low_taps, high_taps = kept[2][:share], kept[2][share:]
        part = jnp.where(first, low_taps, high_taps) + swap(
            jnp.where(first, high_taps, low_taps), 1
        )
        terms = [part] + [
            lax.ppermute(part, "seq", [(i, i ^ m) for i in range(seqs)]) for m in range(1, seqs)
        ]
        while len(terms) > 1:
            terms = [terms[n] + terms[n + 1] for n in range(0, len(terms), 2)]
        total = terms[0]
        backs.append(convolve_back(dlow, dconv, dhigh, conv_kernel, dmixed))
        return (total,), (backs[0],)

    backs = []
    pw_sum, _, (kernel_sum,) = scatter_and_finish(
        lambda m: pw_term[m * size : (m + 1) * size],
        lambda m: (pw_term, m),
        chips,
        (
            (dconv, EDGE, 0),
            (dconv, EDGE, rows // EDGE - 1),
            (kernel_rows, kernel_rows.shape[0], 0),
        ),
        while_pw_travels,
        F32,
    )
    back = backs[0]
    pw_sum = pw_sum.reshape(seqs, piece, width)
    here = lax.axis_index("seq")

    def shard_of(m):
        return lax.dynamic_index_in_dim(pw_sum, here ^ m, 0, keepdims=False)

    pw_grad = shard_of(0)
    for m in range(1, seqs):
        moved = lax.ppermute(
            shard_of(m).astype(BF), "seq", [(i, i ^ m) for i in range(seqs)]
        )
        pw_grad = pw_grad + moved.astype(F32)

    mask = 2
    while mask < count:
        kernel_sum = kernel_sum + swap(kernel_sum, mask)
        mask *= 2
    kernel_got = swap(kernel_sum, 1)
    kernel_grad = jnp.concatenate(
        [
            jnp.where(first, kernel_sum, kernel_got),
            jnp.where(first, kernel_got, kernel_sum)[: taps - share],
        ],
        axis=0,
    )
    return (back[None], kernel_grad, pw_grad, head_grad)


def solution(mesh):
    return jax.shard_map(
        body,
        mesh=mesh,
        in_specs=(
            P("fsdp", "seq", None),
            P(),
            P("fsdp", None),
            P(None, "fsdp"),
            P("fsdp", "seq"),
            P("fsdp", "seq"),
        ),
        out_specs=(P("fsdp", "seq", None), P(), P(("seq", "fsdp"), None), P("seq", "fsdp")),
        check_vma=False,
    )
```

```python
import jax
import jax.numpy as jnp
from jax import lax
from jax.experimental import pallas as pl
from jax.experimental.pallas import tpu as pltpu
from jax.sharding import PartitionSpec as P

BF = jnp.bfloat16
F32 = jnp.float32


def swap(value, mask):
    count = lax.axis_size("fsdp")
    return lax.ppermute(value, "fsdp", [(i, i ^ mask) for i in range(count)])


VMEM_BYTES = 56 * 2**20
CHEAP = pl.CostEstimate(flops=0, bytes_accessed=0, transcendentals=0)


def halves_to_forward(from_x, from_y, *earlier):
    rows, width = from_x.shape
    half = rows // 2

    def kernel(x_ref, y_ref, *refs):
        low_ref, high_ref = refs[len(earlier) :]
        low_ref[...] = x_ref[...]
        high_ref[...] = y_ref[...]

    made = jax.ShapeDtypeStruct((half, width), from_x.dtype)
    whole = pl.BlockSpec((half, width), lambda j: (0, 0))
    return pl.pallas_call(
        kernel,
        grid=(1,),
        out_shape=(made, made),
        in_specs=[
            pl.BlockSpec((half, width), lambda j: (0, 0)),
            pl.BlockSpec((half, width), lambda j: (1, 0)),
        ]
        + [pl.BlockSpec(memory_space=pl.ANY)] * len(earlier),
        out_specs=(whole, whole),
        compiler_params=pltpu.CompilerParams(vmem_limit_bytes=VMEM_BYTES),
        cost_estimate=CHEAP,
        name="forward",
    )(from_x, from_y, *earlier)


def near_and_forward(block, from_x, from_y, *earlier):
    rows, width = block.shape
    half = rows // 2

    def kernel(own_ref, x_ref, y_ref, *refs):
        near_ref, low_ref, high_ref = refs[len(earlier) :]
        near_ref[:rows, :] = own_ref[...]
        near_ref[rows : 2 * rows, :] = x_ref[...]
        near_ref[2 * rows :, :] = y_ref[...]
        low_ref[...] = x_ref[:half, :]
        high_ref[...] = y_ref[half:, :]

    def spec(count):
        return pl.BlockSpec((count, width), lambda j: (0, 0))

    made = jax.ShapeDtypeStruct((half, width), block.dtype)
    return pl.pallas_call(
        kernel,
        grid=(1,),
        out_shape=(jax.ShapeDtypeStruct((3 * rows, width), block.dtype), made, made),
        in_specs=[spec(rows)] * 3 + [pl.BlockSpec(memory_space=pl.ANY)] * len(earlier),
        out_specs=(spec(3 * rows), spec(half), spec(half)),
        compiler_params=pltpu.CompilerParams(vmem_limit_bytes=VMEM_BYTES),
        cost_estimate=CHEAP,
        name="near_and_forward",
    )(block, from_x, from_y, *earlier)


def stack_halves(low, high, *earlier):
    half, width = low.shape

    def kernel(low_ref, high_ref, *refs):
        refs[-1][:half, :] = low_ref[...]
        refs[-1][half:, :] = high_ref[...]

    part = pl.BlockSpec((half, width), lambda j: (0, 0))
    return pl.pallas_call(
        kernel,
        grid=(1,),
        out_shape=jax.ShapeDtypeStruct((2 * half, width), low.dtype),
        in_specs=[part, part] + [pl.BlockSpec(memory_space=pl.ANY)] * len(earlier),
        out_specs=pl.BlockSpec((2 * half, width), lambda j: (0, 0)),
        compiler_params=pltpu.CompilerParams(vmem_limit_bytes=VMEM_BYTES),
        cost_estimate=CHEAP,
        name="stack_halves",
    )(low, high, *earlier)


def gather_rows(block, earlier, between):
    chips = lax.axis_size("fsdp") // 2
    if chips != 4:
        near = jnp.concatenate([block] + [swap(block, 2 * m) for m in range(1, chips - 1)])
        between(near)
        return near, swap(block, 2 * (chips - 1))
    near, to_y, to_x = near_and_forward(block, swap(block, 2), swap(block, 4), *earlier)
    low = swap(to_y, 4)
    high = swap(to_x, 2)
    return near, stack_halves(low, high, *between(near))


def join_halves(near_y, near_x, low, high, earlier, passed=()):
    half, width = low.shape
    rows = 2 * half
    tile = width
    count = len(passed)

    def kernel(y_ref, x_ref, low_ref, high_ref, *refs):
        to_y_ref, to_x_ref = refs[len(earlier) + count : len(earlier) + count + 2]
        to_y_ref[:half, :] = (y_ref[:half, :] + low_ref[...].astype(F32)).astype(BF)
        to_y_ref[half:, :] = y_ref[half:, :].astype(BF)
        to_x_ref[:half, :] = x_ref[:half, :].astype(BF)
        to_x_ref[half:, :] = (x_ref[half:, :] + high_ref[...].astype(F32)).astype(BF)
        for n in range(count):
            refs[len(earlier) + count + 2 + n][...] = refs[n][...]

    def block(size, index):
        return pl.BlockSpec((size, tile), lambda j: (index, j))

    made = jax.ShapeDtypeStruct((rows, width), BF)
    return pl.pallas_call(
        kernel,
        grid=(width // tile,),
        out_shape=(made, made)
        + tuple(jax.ShapeDtypeStruct((size, width), value.dtype) for value, size, _ in passed),
        in_specs=[block(rows, near_y[1]), block(rows, near_x[1]), block(half, 0), block(half, 0)]
        + [block(size, index) for _, size, index in passed]
        + [pl.BlockSpec(memory_space=pl.ANY)] * len(earlier),
        out_specs=(block(rows, 0), block(rows, 0)) + tuple(block(size, 0) for _, size, _ in passed),
        compiler_params=pltpu.CompilerParams(vmem_limit_bytes=VMEM_BYTES),
        cost_estimate=CHEAP,
        name="join_halves",
    )(near_y[0], near_x[0], low, high, *[value for value, _, _ in passed], *earlier)


def gather_pieces(block, *earlier):
    chips = lax.axis_size("fsdp") // 2
    if chips != 4:
        return [(block, 0, 0)] + [(swap(block, 2 * m), m, 0) for m in range(1, chips)]
    half = block.shape[0] // 2
    from_x = swap(block, 2)
    from_y = swap(block, 4)
    if earlier:
        to_y, to_x = halves_to_forward(from_x, from_y, *earlier)
    else:
        to_y, to_x = from_x[:half], from_y[half:]
    far_low = swap(to_y, 4)
    far_high = swap(to_x, 2)
    return [(block, 0, 0), (from_x, 1, 0), (from_y, 2, 0), (far_low, 3, 0), (far_high, 3, half)]


def finish_sum(own, recv_x, recv_y, index, passed, dtype, *earlier):
    rows, width = recv_x.shape
    tile = width
    count = len(passed)

    def kernel(own_ref, x_ref, y_ref, *refs):
        outs = refs[count + len(earlier) :]
        total = own_ref[...] + x_ref[...].astype(F32) + y_ref[...].astype(F32)
        outs[0][...] = total.astype(dtype)
        for n in range(count):
            outs[1 + n][...] = refs[n][...]

    def block(size, at):
        return pl.BlockSpec((size, tile), lambda j: (at, j))

    return pl.pallas_call(
        kernel,
        grid=(width // tile,),
        out_shape=(jax.ShapeDtypeStruct((rows, width), dtype),)
        + tuple(jax.ShapeDtypeStruct(v.shape, v.dtype) for v in passed),
        in_specs=[block(rows, index), block(rows, 0), block(rows, 0)]
        + [block(v.shape[0], 0) for v in passed]
        + [pl.BlockSpec(memory_space=pl.ANY)] * len(earlier),
        out_specs=(block(rows, 0),) + tuple(block(v.shape[0], 0) for v in passed),
        compiler_params=pltpu.CompilerParams(vmem_limit_bytes=VMEM_BYTES),
        cost_estimate=CHEAP,
        name="finish_sum",
    )(own, recv_x, recv_y, *passed, *earlier)


def scatter_and_finish(part, near, chips, passed, last, dtype):
    if chips != 4:
        total = part(0)
        for m in range(1, chips):
            total = total + swap(part(m).astype(BF), 2 * m).astype(F32)
        kept = [v[size * index : size * (index + 1)] for v, size, index in passed]
        return total.astype(dtype), kept, last(kept, total)[0]
    far = part(3).astype(BF)
    half = far.shape[0] // 2
    low = swap(far[:half], 2)
    high = swap(far[half:], 4)
    own, index = near(0)
    to_y, to_x, *kept = join_halves(near(2), near(1), low, high, (own,), passed)
    recv_x, recv_y = swap(to_x, 2), swap(to_y, 4)
    handed, waited = last(kept, to_x)
    total, *handed = finish_sum(own, recv_x, recv_y, index, handed, dtype, *waited)
    return total, kept, handed


def project(gated, frames, pieces, places):
    rows, width = gated.shape
    count = len(pieces)
    tile = 512

    def kernel(*refs):
        place = refs[0]
        gated_ref, frames_ref = refs[1:3]
        piece_refs = refs[3 : 3 + count]
        mixed_ref, full_ref, held, sems, out_sem = refs[3 + count :]
        copies = []
        for n in range(count):
            size = piece_refs[n].shape[0]
            start = pl.multiple_of(place[n], 16)
            copy = pltpu.make_async_copy(piece_refs[n], held.at[pl.ds(start, size)], sems.at[n])
            copy.start()
            copies.append(copy)
        for copy in copies:
            copy.wait()
        out = pltpu.make_async_copy(held, full_ref, out_sem)
        out.start()
        for col in range(0, width, tile):
            at = slice(col, col + tile)
            proj = jnp.dot(gated_ref[...], held[:, at], preferred_element_type=F32)
            mixed_ref[:, at] = (frames_ref[:, at].astype(F32) + proj).astype(BF)
        out.wait()

    vmem = pl.BlockSpec(memory_space=pltpu.VMEM)
    hbm = pl.BlockSpec(memory_space=pl.ANY)
    return pl.pallas_call(
        kernel,
        out_shape=(
            jax.ShapeDtypeStruct((rows, width), BF),
            jax.ShapeDtypeStruct((width, width), BF),
        ),
        in_specs=[pl.BlockSpec(memory_space=pltpu.SMEM), vmem, vmem] + [hbm] * count,
        out_specs=(vmem, hbm),
        scratch_shapes=[
            pltpu.VMEM((width, width), BF),
            pltpu.SemaphoreType.DMA((count,)),
            pltpu.SemaphoreType.DMA,
        ],
        compiler_params=pltpu.CompilerParams(vmem_limit_bytes=VMEM_BYTES),
        cost_estimate=pl.CostEstimate(
            flops=2 * rows * width * width, bytes_accessed=4 * width * width, transcendentals=0
        ),
        name="project",
    )(places, gated, frames, *pieces)


def line_scatter(term, kind):
    count = lax.axis_size("seq")
    here = lax.axis_index("seq")

    def block(index):
        index = jnp.clip(index, 0, count - 1)
        return lax.dynamic_index_in_dim(term, index, 0, keepdims=False).astype(F32)

    up = down = None
    for step in range(1, count):
        to_up = block(here + count - step)
        to_down = block(here - count + step)
        if up is not None:
            to_up = to_up + up.astype(F32)
            to_down = to_down + down.astype(F32)
        up = lax.ppermute(to_up.astype(kind), "seq", [(i, i + 1) for i in range(step)])
        down = lax.ppermute(
            to_down.astype(kind), "seq", [(i, i - 1) for i in range(count - step, count)]
        )
    return block(here) + up.astype(F32) + down.astype(F32)


def halo_edges(first, last):
    count = lax.axis_size("seq")
    forward = [(i, i + 1) for i in range(count - 1)]
    backward = [(i + 1, i) for i in range(count - 1)]
    return lax.ppermute(last, "seq", forward), lax.ppermute(first, "seq", backward)


EDGE = 16
LOGIT_TILE = 512
LANES = 128


def channel_tile(width):
    return 256 if width % 256 == 0 else width


def fill(pad_ref, shifted_ref, low_ref, mid_ref, high_ref):
    rows = mid_ref.shape[0]
    pad_ref[:EDGE, :] = low_ref[...].astype(F32)
    pad_ref[EDGE : EDGE + rows, :] = mid_ref[...].astype(F32)
    pad_ref[EDGE + rows :, :] = high_ref[...].astype(F32)
    for shift in range(8):
        shifted_ref[shift] = pad_ref[shift : shift + rows + 24, :]


def tap_rows(shifted_ref, start, rows, at):
    shift = start % 8
    return shifted_ref[shift, start - shift : start - shift + rows, at]


def pad_scratch(rows, tile):
    return [
        pltpu.VMEM((rows + 2 * EDGE, tile), F32),
        pltpu.VMEM((8, rows + 24, tile), F32),
    ]


def tap_specs(rows, tile):
    edge = pl.BlockSpec((EDGE, tile), lambda j: (0, j))
    return edge, pl.BlockSpec((rows, tile), lambda j: (0, j))


def convolve(low, frames, high, taps):
    rows, width = frames.shape
    count = taps.shape[0]
    first = EDGE - (count - 1) // 2
    tile = channel_tile(width)

    def kernel(
        low_ref, mid_ref, high_ref, taps_ref, conv_ref, gated_ref, turned_ref, mark_ref, pad_ref, shifted_ref
    ):
        mark_ref[...] = jnp.zeros_like(mark_ref)
        fill(pad_ref, shifted_ref, low_ref, mid_ref, high_ref)
        for lane in range(0, tile, LANES):
            at = slice(lane, lane + LANES)
            conv = jnp.zeros((rows, LANES), F32)
            for k in range(count):
                conv = conv + taps_ref[k : k + 1, at] * tap_rows(shifted_ref, first + k, rows, at)
            conv_ref[:, at] = conv
            gated = conv / (1.0 + jnp.exp(-conv))
            gated_ref[:, at] = gated.astype(BF)
            turned_ref[at, :] = gated.T.astype(BF)

    edge, body_spec = tap_specs(rows, tile)
    return pl.pallas_call(
        kernel,
        grid=(width // tile,),
        out_shape=(
            jax.ShapeDtypeStruct((rows, width), F32),
            jax.ShapeDtypeStruct((rows, width), BF),
            jax.ShapeDtypeStruct((width, rows), BF),
            jax.ShapeDtypeStruct((8, LANES), F32),
        ),
        in_specs=[edge, body_spec, edge, pl.BlockSpec((count, tile), lambda j: (0, j))],
        out_specs=(
            body_spec,
            body_spec,
            pl.BlockSpec((tile, rows), lambda j: (j, 0)),
            pl.BlockSpec((8, LANES), lambda j: (0, 0)),
        ),
        scratch_shapes=pad_scratch(rows, tile),
        compiler_params=pltpu.CompilerParams(vmem_limit_bytes=VMEM_BYTES),
        cost_estimate=CHEAP,
        name="convolve",
    )(low, frames, high, taps)


def convolve_back(low, dconv, high, taps, dmixed):
    rows, width = dconv.shape
    count = taps.shape[0]
    last = EDGE + (count - 1) // 2
    tile = channel_tile(width)

    def kernel(low_ref, mid_ref, high_ref, taps_ref, dmixed_ref, out_ref, pad_ref, shifted_ref):
        fill(pad_ref, shifted_ref, low_ref, mid_ref, high_ref)
        for lane in range(0, tile, LANES):
            at = slice(lane, lane + LANES)
            back = dmixed_ref[:, at].astype(F32)
            for k in range(count):
                back = back + taps_ref[k : k + 1, at] * tap_rows(shifted_ref, last - k, rows, at)
            out_ref[:, at] = back.astype(BF)

    edge, body_spec = tap_specs(rows, tile)
    return pl.pallas_call(
        kernel,
        grid=(width // tile,),
        out_shape=jax.ShapeDtypeStruct((rows, width), BF),
        in_specs=[edge, body_spec, edge, pl.BlockSpec((count, tile), lambda j: (0, j)), body_spec],
        out_specs=body_spec,
        scratch_shapes=pad_scratch(rows, tile),
        compiler_params=pltpu.CompilerParams(vmem_limit_bytes=VMEM_BYTES),
        cost_estimate=CHEAP,
        name="convolve_back",
    )(low, dconv, high, taps, dmixed)


def gate_back(dmixed, pw_full, conv, low, frames, high, count, earlier):
    rows, width = dmixed.shape
    first = EDGE - (count - 1) // 2
    tile = channel_tile(width)
    held = -(-count // 16) * 16

    def kernel(
        dmixed_ref, pw_ref, conv_ref, low_ref, mid_ref, high_ref, _, dconv_ref, taps_ref, pad_ref,
        shifted_ref,
    ):
        fill(pad_ref, shifted_ref, low_ref, mid_ref, high_ref)
        dgated = lax.dot_general(
            dmixed_ref[...], pw_ref[...], (((1,), (1,)), ((), ())), preferred_element_type=F32
        )
        conv = conv_ref[...]
        sig = 1.0 / (1.0 + jnp.exp(-conv))
        dconv_ref[...] = (dgated * sig * (1.0 + conv * (1.0 - sig))).astype(BF)
        taps_ref[...] = jnp.zeros_like(taps_ref)
        for lane in range(0, tile, LANES):
            at = slice(lane, lane + LANES)
            dconv = dconv_ref[:, at].astype(F32)
            for k in range(count):
                term = dconv * tap_rows(shifted_ref, first + k, rows, at)
                taps_ref[k : k + 1, at] = jnp.sum(term, axis=0, keepdims=True)

    edge, body_spec = tap_specs(rows, tile)
    return pl.pallas_call(
        kernel,
        grid=(width // tile,),
        out_shape=(
            jax.ShapeDtypeStruct((rows, width), BF),
            jax.ShapeDtypeStruct((held, width), F32),
        ),
        in_specs=[
            pl.BlockSpec((rows, width), lambda j: (0, 0)),
            pl.BlockSpec((tile, width), lambda j: (j, 0)),
            body_spec,
            edge,
            body_spec,
            edge,
            pl.BlockSpec(memory_space=pl.ANY),
        ],
        out_specs=(body_spec, pl.BlockSpec((held, tile), lambda j: (0, j))),
        scratch_shapes=pad_scratch(rows, tile),
        compiler_params=pltpu.CompilerParams(vmem_limit_bytes=VMEM_BYTES),
        cost_estimate=pl.CostEstimate(
            flops=6 * 10**9, bytes_accessed=44 * 10**6, transcendentals=0
        ),
        name="gate_back",
    )(dmixed, pw_full, conv, low, frames, high, earlier)


def head_terms(left_own, left_other, right_own, right_other, earlier):
    width = left_own[0].shape[1]
    depth, vocab = right_own.shape
    split = left_own[0].shape[0]
    tile = channel_tile(width)

    def kernel(near_a, far_a, near_b, far_b, ra_ref, rb_ref, _, out_ref):
        lhs = (((0,), (0,)), ((), ()))
        term = jnp.zeros(out_ref.shape, F32)
        for near, far, right in ((near_a, far_a, ra_ref), (near_b, far_b, rb_ref)):
            term += lax.dot_general(near[...], right[:split], lhs, preferred_element_type=F32)
            term += lax.dot_general(far[...], right[split:], lhs, preferred_element_type=F32)
        out_ref[...] = term.astype(BF)

    near = pl.BlockSpec((split, tile), lambda j: (0, j))
    far = pl.BlockSpec((depth - split, tile), lambda j: (0, j))
    right = pl.BlockSpec((depth, vocab), lambda j: (0, 0))
    return pl.pallas_call(
        kernel,
        grid=(width // tile,),
        out_shape=jax.ShapeDtypeStruct((width, vocab), BF),
        in_specs=[near, far, near, far, right, right, pl.BlockSpec(memory_space=pl.ANY)],
        out_specs=pl.BlockSpec((tile, vocab), lambda j: (j, 0)),
        compiler_params=pltpu.CompilerParams(vmem_limit_bytes=VMEM_BYTES),
        cost_estimate=pl.CostEstimate(
            flops=13 * 10**9, bytes_accessed=40 * 10**6, transcendentals=0
        ),
        name="head_terms",
    )(*left_own, *left_other, right_own, right_other, earlier)


def logits_and_stats(mixed, head, other):
    rows, width = mixed.shape
    vocab = head.shape[1]
    tile = min(LOGIT_TILE, vocab)
    steps = vocab // tile

    def kernel(x_ref, a_ref, b_ref, la_ref, lb_ref, stats_ref, top_ref, total_ref):
        step = pl.program_id(0)

        @pl.when(step == 0)
        def _():
            top_ref[...] = jnp.full_like(top_ref, -jnp.inf)
            total_ref[...] = jnp.zeros_like(total_ref)

        la_ref[...] = jnp.dot(x_ref[...], a_ref[...], preferred_element_type=F32)
        lb_ref[...] = jnp.dot(x_ref[...], b_ref[...], preferred_element_type=F32)
        parts = [
            ref[:, lane : lane + LANES] for ref in (la_ref, lb_ref) for lane in range(0, tile, LANES)
        ]
        old = top_ref[...]
        new = old
        for part in parts:
            new = jnp.maximum(new, part)
        total = total_ref[...] * jnp.exp(old - new)
        for part in parts:
            total = total + jnp.exp(part - new)
        top_ref[...] = new
        total_ref[...] = total

        @pl.when(step == steps - 1)
        def _():
            tops, totals = new.T, total.T
            top = jnp.max(tops, axis=0, keepdims=True)
            total_row = jnp.sum(totals * jnp.exp(tops - top), axis=0, keepdims=True)
            row = lax.broadcasted_iota(jnp.int32, (8, rows), 0)
            stats_ref[...] = jnp.where(row == 0, top, total_row)

    columns = pl.BlockSpec((width, tile), lambda j: (0, j))
    made = pl.BlockSpec((rows, tile), lambda j: (0, j))
    return pl.pallas_call(
        kernel,
        grid=(steps,),
        out_shape=(
            jax.ShapeDtypeStruct((rows, vocab), F32),
            jax.ShapeDtypeStruct((rows, vocab), F32),
            jax.ShapeDtypeStruct((8, rows), F32),
        ),
        in_specs=[pl.BlockSpec((rows, width), lambda j: (0, 0)), columns, columns],
        out_specs=(made, made, pl.BlockSpec((8, rows), lambda j: (0, 0))),
        scratch_shapes=[pltpu.VMEM((rows, 128), F32), pltpu.VMEM((rows, 128), F32)],
        compiler_params=pltpu.CompilerParams(vmem_limit_bytes=VMEM_BYTES),
        cost_estimate=pl.CostEstimate(flops=0, bytes_accessed=0, transcendentals=0),
        name="logits",
    )(mixed, head, other)


def logit_gradients(firsts, near, far, stats, labels):
    chips = len(stats)
    rows, vocab = far[0].shape
    tile = min(LOGIT_TILE, vocab)

    def kernel(*refs):
        first_ref = refs[0]
        logit_refs = [refs[1 + 2 * m : 3 + 2 * m] for m in range(chips)]
        stat_refs = refs[1 + 2 * chips : 1 + 3 * chips]
        label_refs = refs[1 + 3 * chips : 1 + 4 * chips]
        own_ref, other_ref, columns_ref = refs[1 + 4 * chips :]
        step = pl.program_id(0)

        @pl.when(step == 0)
        def _():
            for m in range(chips):
                tops, totals = [], []
                for o in range(chips):
                    at = m ^ o
                    tops.append(stat_refs[o][at : at + 1, :])
                    totals.append(stat_refs[o][chips + at : chips + at + 1, :])
                top = tops[0]
                for t in tops[1:]:
                    top = jnp.maximum(top, t)
                total = sum(s * jnp.exp(t - top) for s, t in zip(totals, tops))
                values = jnp.concatenate(
                    [
                        top,
                        1.0 / total,
                        label_refs[m][0:1, :],
                        label_refs[m][1:2, :],
                        jnp.zeros((124, rows), F32),
                    ],
                    axis=0,
                )
                columns_ref[m] = values.T

        entries = lax.broadcasted_iota(jnp.int32, (rows, tile), 1) + step * tile
        for m in range(chips):
            columns = columns_ref[m]
            top, inverse = columns[:, 0:1], columns[:, 1:2]
            target = columns[:, 2:3].astype(jnp.int32)
            weight = columns[:, 3:4]
            for k, out_ref in enumerate((own_ref, other_ref)):
                probs = jnp.exp(logit_refs[m][k][...] - top) * inverse
                hit = (entries == target - first_ref[k]).astype(F32)
                out_ref[m * rows : (m + 1) * rows, :] = (weight * (probs - hit)).astype(BF)

    def block(index):
        return pl.BlockSpec((rows, tile), lambda j: (index, j))

    made = pl.BlockSpec((chips * rows, tile), lambda j: (0, j))
    return pl.pallas_call(
        kernel,
        grid=(vocab // tile,),
        out_shape=(
            jax.ShapeDtypeStruct((chips * rows, vocab), BF),
            jax.ShapeDtypeStruct((chips * rows, vocab), BF),
        ),
        in_specs=[pl.BlockSpec(memory_space=pltpu.SMEM)]
        + [block(m) for m in range(chips - 1) for _ in range(2)]
        + [block(0)] * 2
        + [pl.BlockSpec((2 * chips, rows), lambda j: (0, 0))] * chips
        + [pl.BlockSpec((2, rows), lambda j: (0, 0))] * chips,
        out_specs=(made, made),
        scratch_shapes=[pltpu.VMEM((chips, rows, 128), F32)],
        compiler_params=pltpu.CompilerParams(vmem_limit_bytes=VMEM_BYTES),
        cost_estimate=pl.CostEstimate(flops=0, bytes_accessed=0, transcendentals=0),
        name="dlogits",
    )(firsts, *(list(near) * (chips - 1)), *far, *stats, *labels)


def body(frames, conv_kernel, pw_weight, head_weight, targets, frame_weight):
    frames = frames[0]
    rows, width = frames.shape
    taps = conv_kernel.shape[0]
    seqs = lax.axis_size("seq")
    count = lax.axis_size("fsdp")
    chips = count // 2
    me = lax.axis_index("fsdp")
    chip = me // 2
    core = me % 2
    low, high = halo_edges(frames[:EDGE], frames[-EDGE:])
    conv, gated, turned, mark = convolve(low, frames, high, conv_kernel)
    shard = pw_weight.shape[0]
    pieces, places = [], []
    gathered = gather_pieces(pw_weight, mark)
    for piece, m, first in gathered:
        pieces += [piece, swap(piece, 1)]
        places += [(me ^ (2 * m)) * shard + first, (me ^ (2 * m + 1)) * shard + first]
    places = jnp.stack(places).astype(jnp.int32)
    head_other = swap(head_weight, 1)

    mixed, pw_full = project(gated, frames, pieces, places)
    labels = jnp.stack([targets[0].astype(F32), frame_weight[0].astype(F32)])
    all_labels = [labels] + [swap(labels, 2 * m) for m in range(1, chips)]

    piece = width // (seqs * count)
    gated_t = turned.reshape(seqs, chips, 2, piece, rows)
    gated_t = jnp.stack(
        [lax.dynamic_index_in_dim(gated_t, chip ^ m, 1, keepdims=False) for m in range(chips)]
    )
    gated_own = lax.dynamic_index_in_dim(gated_t, core, 2, keepdims=False)
    gated_sent = lax.dynamic_index_in_dim(gated_t, 1 - core, 2, keepdims=False)
    gated_got = swap(gated_sent, 1)
    gated_pair = jnp.concatenate([gated_own, gated_got], axis=-1)

    weights = (head_weight, head_other)
    vocab = head_weight.shape[1]
    pairs, tops, totals = [], [], []

    def near_logits(block):
        own, other, stats = logits_and_stats(block, *weights)
        pairs.append((own, other))
        tops.append(stats[0].reshape(-1, rows))
        totals.append(stats[1].reshape(-1, rows))
        return (stats,)

    near_own, far_own = gather_rows(mixed, (gated_got,), near_logits)
    pair = [jnp.dot(far_own, w, preferred_element_type=F32) for w in weights]
    top = jnp.maximum(jnp.max(pair[0], axis=1), jnp.max(pair[1], axis=1))
    total = sum(jnp.sum(jnp.exp(l - top[:, None]), axis=1) for l in pair)
    pairs.append(pair)
    tops.append(top.reshape(-1, rows))
    totals.append(total.reshape(-1, rows))
    near_other = swap(near_own, 1)
    far_other = swap(far_own, 1)
    packed = jnp.concatenate(tops + totals)
    got = [packed] + [swap(packed, 2 * m) for m in range(1, chips)]
    firsts = jnp.stack([me * vocab, (me ^ 1) * vocab]).astype(jnp.int32)
    right_own, right_sent = logit_gradients(firsts, pairs[0], pairs[1], got, all_labels)
    right_other = swap(right_sent, 1)

    def back_head(m):
        rhs = (((1,), (1,)), ((), ()))
        at = slice(m * rows, (m + 1) * rows)
        return lax.dot_general(
            right_own[at], head_weight, rhs, preferred_element_type=F32
        ) + lax.dot_general(right_sent[at], head_other, rhs, preferred_element_type=F32)

    terms = []

    def while_dmixed_travels(_, sent):
        terms.append(
            head_terms((near_own, far_own), (near_other, far_other), right_own, right_other, sent)
        )
        return (), (terms[0],)

    dmixed, _, _ = scatter_and_finish(
        back_head, lambda m: (back_head(m), 0), chips, (), while_dmixed_travels, BF
    )
    head_grad = lax.psum_scatter(terms[0], "seq", scatter_dimension=0, tiled=True).astype(F32)

    dmixed_pair = jnp.concatenate([dmixed, swap(dmixed, 1)], axis=0)
    pw_term = jnp.dot(
        gated_pair.reshape(-1, 2 * rows), dmixed_pair, preferred_element_type=F32
    )
    dconv, kernel_rows = gate_back(
        dmixed, pw_full, conv, low, frames, high, taps, pw_term[:8, :LANES]
    )
    size = seqs * piece
    first = core == 0
    share = kernel_rows.shape[0] // 2

    def while_pw_travels(kept, _):
        dlow, dhigh = halo_edges(*kept[:2])
        low_taps, high_taps = kept[2][:share], kept[2][share:]
        part = jnp.where(first, low_taps, high_taps) + swap(
            jnp.where(first, high_taps, low_taps), 1
        )
        terms = [part] + [
            lax.ppermute(part, "seq", [(i, i ^ m) for i in range(seqs)]) for m in range(1, seqs)
        ]
        while len(terms) > 1:
            terms = [terms[n] + terms[n + 1] for n in range(0, len(terms), 2)]
        total = terms[0]
        backs.append(convolve_back(dlow, dconv, dhigh, conv_kernel, dmixed))
        return (total,), (backs[0],)

    backs = []
    pw_sum, _, (kernel_sum,) = scatter_and_finish(
        lambda m: pw_term[m * size : (m + 1) * size],
        lambda m: (pw_term, m),
        chips,
        (
            (dconv, EDGE, 0),
            (dconv, EDGE, rows // EDGE - 1),
            (kernel_rows, kernel_rows.shape[0], 0),
        ),
        while_pw_travels,
        F32,
    )
    back = backs[0]
    pw_sum = pw_sum.reshape(seqs, piece, width)
    here = lax.axis_index("seq")

    def shard_of(m):
        return lax.dynamic_index_in_dim(pw_sum, here ^ m, 0, keepdims=False)

    pw_grad = shard_of(0)
    for m in range(1, seqs):
        moved = lax.ppermute(
            shard_of(m).astype(BF), "seq", [(i, i ^ m) for i in range(seqs)]
        )
        pw_grad = pw_grad + moved.astype(F32)

    mask = 2
    while mask < count:
        kernel_sum = kernel_sum + swap(kernel_sum, mask)
        mask *= 2
    kernel_got = swap(kernel_sum, 1)
    kernel_grad = jnp.concatenate(
        [
            jnp.where(first, kernel_sum, kernel_got),
            jnp.where(first, kernel_got, kernel_sum)[: taps - share],
        ],
        axis=0,
    )
    return (back[None], kernel_grad, pw_grad, head_grad)


def solution(mesh):
    return jax.shard_map(
        body,
        mesh=mesh,
        in_specs=(
            P("fsdp", "seq", None),
            P(),
            P("fsdp", None),
            P(None, "fsdp"),
            P("fsdp", "seq"),
            P("fsdp", "seq"),
        ),
        out_specs=(P("fsdp", "seq", None), P(), P(("seq", "fsdp"), None), P("seq", "fsdp")),
        check_vma=False,
    )
```

```python
import jax
import jax.numpy as jnp
from jax import lax
from jax.experimental import pallas as pl
from jax.experimental.pallas import tpu as pltpu
from jax.sharding import PartitionSpec as P

BF = jnp.bfloat16
F32 = jnp.float32


def swap(value, mask):
    count = lax.axis_size("fsdp")
    return lax.ppermute(value, "fsdp", [(i, i ^ mask) for i in range(count)])


VMEM_BYTES = 56 * 2**20
CHEAP = pl.CostEstimate(flops=0, bytes_accessed=0, transcendentals=0)


def halves_to_forward(from_x, from_y, *earlier):
    rows, width = from_x.shape
    half = rows // 2

    def kernel(x_ref, y_ref, *refs):
        low_ref, high_ref = refs[len(earlier) :]
        low_ref[...] = x_ref[...]
        high_ref[...] = y_ref[...]

    made = jax.ShapeDtypeStruct((half, width), from_x.dtype)
    whole = pl.BlockSpec((half, width), lambda j: (0, 0))
    return pl.pallas_call(
        kernel,
        grid=(1,),
        out_shape=(made, made),
        in_specs=[
            pl.BlockSpec((half, width), lambda j: (0, 0)),
            pl.BlockSpec((half, width), lambda j: (1, 0)),
        ]
        + [pl.BlockSpec(memory_space=pl.ANY)] * len(earlier),
        out_specs=(whole, whole),
        compiler_params=pltpu.CompilerParams(vmem_limit_bytes=VMEM_BYTES),
        cost_estimate=CHEAP,
        name="forward",
    )(from_x, from_y, *earlier)


def near_and_forward(block, from_x, from_y, *earlier):
    rows, width = block.shape
    half = rows // 2

    def kernel(own_ref, x_ref, y_ref, *refs):
        near_ref, low_ref, high_ref = refs[len(earlier) :]
        near_ref[:rows, :] = own_ref[...]
        near_ref[rows : 2 * rows, :] = x_ref[...]
        near_ref[2 * rows :, :] = y_ref[...]
        low_ref[...] = x_ref[:half, :]
        high_ref[...] = y_ref[half:, :]

    def spec(count):
        return pl.BlockSpec((count, width), lambda j: (0, 0))

    made = jax.ShapeDtypeStruct((half, width), block.dtype)
    return pl.pallas_call(
        kernel,
        grid=(1,),
        out_shape=(jax.ShapeDtypeStruct((3 * rows, width), block.dtype), made, made),
        in_specs=[spec(rows)] * 3 + [pl.BlockSpec(memory_space=pl.ANY)] * len(earlier),
        out_specs=(spec(3 * rows), spec(half), spec(half)),
        compiler_params=pltpu.CompilerParams(vmem_limit_bytes=VMEM_BYTES),
        cost_estimate=CHEAP,
        name="near_and_forward",
    )(block, from_x, from_y, *earlier)


def stack_halves(low, high, *earlier):
    half, width = low.shape

    def kernel(low_ref, high_ref, *refs):
        refs[-1][:half, :] = low_ref[...]
        refs[-1][half:, :] = high_ref[...]

    part = pl.BlockSpec((half, width), lambda j: (0, 0))
    return pl.pallas_call(
        kernel,
        grid=(1,),
        out_shape=jax.ShapeDtypeStruct((2 * half, width), low.dtype),
        in_specs=[part, part] + [pl.BlockSpec(memory_space=pl.ANY)] * len(earlier),
        out_specs=pl.BlockSpec((2 * half, width), lambda j: (0, 0)),
        compiler_params=pltpu.CompilerParams(vmem_limit_bytes=VMEM_BYTES),
        cost_estimate=CHEAP,
        name="stack_halves",
    )(low, high, *earlier)


def gather_rows(block, earlier, between):
    chips = lax.axis_size("fsdp") // 2
    if chips != 4:
        near = jnp.concatenate([block] + [swap(block, 2 * m) for m in range(1, chips - 1)])
        between(near)
        return near, swap(block, 2 * (chips - 1))
    near, to_y, to_x = near_and_forward(block, swap(block, 2), swap(block, 4), *earlier)
    low = swap(to_y, 4)
    high = swap(to_x, 2)
    return near, stack_halves(low, high, *between(near))


def join_halves(near_y, near_x, low, high, earlier, passed=()):
    half, width = low.shape
    rows = 2 * half
    tile = width
    count = len(passed)

    def kernel(y_ref, x_ref, low_ref, high_ref, *refs):
        to_y_ref, to_x_ref = refs[len(earlier) + count : len(earlier) + count + 2]
        to_y_ref[:half, :] = (y_ref[:half, :] + low_ref[...].astype(F32)).astype(BF)
        to_y_ref[half:, :] = y_ref[half:, :].astype(BF)
        to_x_ref[:half, :] = x_ref[:half, :].astype(BF)
        to_x_ref[half:, :] = (x_ref[half:, :] + high_ref[...].astype(F32)).astype(BF)
        for n in range(count):
            refs[len(earlier) + count + 2 + n][...] = refs[n][...]

    def block(size, index):
        return pl.BlockSpec((size, tile), lambda j: (index, j))

    made = jax.ShapeDtypeStruct((rows, width), BF)
    return pl.pallas_call(
        kernel,
        grid=(width // tile,),
        out_shape=(made, made)
        + tuple(jax.ShapeDtypeStruct((size, width), value.dtype) for value, size, _ in passed),
        in_specs=[block(rows, near_y[1]), block(rows, near_x[1]), block(half, 0), block(half, 0)]
        + [block(size, index) for _, size, index in passed]
        + [pl.BlockSpec(memory_space=pl.ANY)] * len(earlier),
        out_specs=(block(rows, 0), block(rows, 0)) + tuple(block(size, 0) for _, size, _ in passed),
        compiler_params=pltpu.CompilerParams(vmem_limit_bytes=VMEM_BYTES),
        cost_estimate=CHEAP,
        name="join_halves",
    )(near_y[0], near_x[0], low, high, *[value for value, _, _ in passed], *earlier)


def gather_pieces(block, *earlier):
    chips = lax.axis_size("fsdp") // 2
    if chips != 4:
        return [(block, 0, 0)] + [(swap(block, 2 * m), m, 0) for m in range(1, chips)]
    half = block.shape[0] // 2
    from_x = swap(block, 2)
    from_y = swap(block, 4)
    if earlier:
        to_y, to_x = halves_to_forward(from_x, from_y, *earlier)
    else:
        to_y, to_x = from_x[:half], from_y[half:]
    far_low = swap(to_y, 4)
    far_high = swap(to_x, 2)
    return [(block, 0, 0), (from_x, 1, 0), (from_y, 2, 0), (far_low, 3, 0), (far_high, 3, half)]


def finish_sum(own, recv_x, recv_y, index, passed, dtype, *earlier):
    rows, width = recv_x.shape
    tile = width
    count = len(passed)

    def kernel(own_ref, x_ref, y_ref, *refs):
        outs = refs[count + len(earlier) :]
        total = own_ref[...] + x_ref[...].astype(F32) + y_ref[...].astype(F32)
        outs[0][...] = total.astype(dtype)
        for n in range(count):
            outs[1 + n][...] = refs[n][...]

    def block(size, at):
        return pl.BlockSpec((size, tile), lambda j: (at, j))

    return pl.pallas_call(
        kernel,
        grid=(width // tile,),
        out_shape=(jax.ShapeDtypeStruct((rows, width), dtype),)
        + tuple(jax.ShapeDtypeStruct(v.shape, v.dtype) for v in passed),
        in_specs=[block(rows, index), block(rows, 0), block(rows, 0)]
        + [block(v.shape[0], 0) for v in passed]
        + [pl.BlockSpec(memory_space=pl.ANY)] * len(earlier),
        out_specs=(block(rows, 0),) + tuple(block(v.shape[0], 0) for v in passed),
        compiler_params=pltpu.CompilerParams(vmem_limit_bytes=VMEM_BYTES),
        cost_estimate=CHEAP,
        name="finish_sum",
    )(own, recv_x, recv_y, *passed, *earlier)


def scatter_and_finish(part, near, chips, passed, last, dtype):
    if chips != 4:
        total = part(0)
        for m in range(1, chips):
            total = total + swap(part(m).astype(BF), 2 * m).astype(F32)
        kept = [v[size * index : size * (index + 1)] for v, size, index in passed]
        return total.astype(dtype), kept, last(kept, total)[0]
    far = part(3).astype(BF)
    half = far.shape[0] // 2
    low = swap(far[:half], 2)
    high = swap(far[half:], 4)
    own, index = near(0)
    to_y, to_x, *kept = join_halves(near(2), near(1), low, high, (own,), passed)
    recv_x, recv_y = swap(to_x, 2), swap(to_y, 4)
    handed, waited = last(kept, to_x)
    total, *handed = finish_sum(own, recv_x, recv_y, index, handed, dtype, *waited)
    return total, kept, handed


def project(gated, frames, pieces, places):
    rows, width = gated.shape
    count = len(pieces)
    tile = 512

    def kernel(*refs):
        place = refs[0]
        gated_ref, frames_ref = refs[1:3]
        piece_refs = refs[3 : 3 + count]
        mixed_ref, full_ref, held, sems, out_sem = refs[3 + count :]
        copies = []
        for n in range(count):
            size = piece_refs[n].shape[0]
            start = pl.multiple_of(place[n], 16)
            copy = pltpu.make_async_copy(piece_refs[n], held.at[pl.ds(start, size)], sems.at[n])
            copy.start()
            copies.append(copy)
        for copy in copies:
            copy.wait()
        out = pltpu.make_async_copy(held, full_ref, out_sem)
        out.start()
        for col in range(0, width, tile):
            at = slice(col, col + tile)
            proj = jnp.dot(gated_ref[...], held[:, at], preferred_element_type=F32)
            mixed_ref[:, at] = (frames_ref[:, at].astype(F32) + proj).astype(BF)
        out.wait()

    vmem = pl.BlockSpec(memory_space=pltpu.VMEM)
    hbm = pl.BlockSpec(memory_space=pl.ANY)
    return pl.pallas_call(
        kernel,
        out_shape=(
            jax.ShapeDtypeStruct((rows, width), BF),
            jax.ShapeDtypeStruct((width, width), BF),
        ),
        in_specs=[pl.BlockSpec(memory_space=pltpu.SMEM), vmem, vmem] + [hbm] * count,
        out_specs=(vmem, hbm),
        scratch_shapes=[
            pltpu.VMEM((width, width), BF),
            pltpu.SemaphoreType.DMA((count,)),
            pltpu.SemaphoreType.DMA,
        ],
        compiler_params=pltpu.CompilerParams(vmem_limit_bytes=VMEM_BYTES),
        cost_estimate=pl.CostEstimate(
            flops=2 * rows * width * width, bytes_accessed=4 * width * width, transcendentals=0
        ),
        name="project",
    )(places, gated, frames, *pieces)


def line_scatter(term, kind):
    count = lax.axis_size("seq")
    here = lax.axis_index("seq")

    def block(index):
        index = jnp.clip(index, 0, count - 1)
        return lax.dynamic_index_in_dim(term, index, 0, keepdims=False).astype(F32)

    up = down = None
    for step in range(1, count):
        to_up = block(here + count - step)
        to_down = block(here - count + step)
        if up is not None:
            to_up = to_up + up.astype(F32)
            to_down = to_down + down.astype(F32)
        up = lax.ppermute(to_up.astype(kind), "seq", [(i, i + 1) for i in range(step)])
        down = lax.ppermute(
            to_down.astype(kind), "seq", [(i, i - 1) for i in range(count - step, count)]
        )
    return block(here) + up.astype(F32) + down.astype(F32)


def halo_edges(first, last):
    count = lax.axis_size("seq")
    forward = [(i, i + 1) for i in range(count - 1)]
    backward = [(i + 1, i) for i in range(count - 1)]
    return lax.ppermute(last, "seq", forward), lax.ppermute(first, "seq", backward)


EDGE = 16
LOGIT_TILE = 512
LANES = 128


def channel_tile(width):
    return 384 if width % 384 == 0 else width


def fill(pad_ref, shifted_ref, low_ref, mid_ref, high_ref):
    rows = mid_ref.shape[0]
    pad_ref[:EDGE, :] = low_ref[...].astype(F32)
    pad_ref[EDGE : EDGE + rows, :] = mid_ref[...].astype(F32)
    pad_ref[EDGE + rows :, :] = high_ref[...].astype(F32)
    for shift in range(8):
        shifted_ref[shift] = pad_ref[shift : shift + rows + 24, :]


def tap_rows(shifted_ref, start, rows, at):
    shift = start % 8
    return shifted_ref[shift, start - shift : start - shift + rows, at]


def pad_scratch(rows, tile):
    return [
        pltpu.VMEM((rows + 2 * EDGE, tile), F32),
        pltpu.VMEM((8, rows + 24, tile), F32),
    ]


def tap_specs(rows, tile):
    edge = pl.BlockSpec((EDGE, tile), lambda j: (0, j))
    return edge, pl.BlockSpec((rows, tile), lambda j: (0, j))


def convolve(low, frames, high, taps):
    rows, width = frames.shape
    count = taps.shape[0]
    first = EDGE - (count - 1) // 2
    tile = channel_tile(width)

    def kernel(
        low_ref, mid_ref, high_ref, taps_ref, conv_ref, gated_ref, turned_ref, mark_ref, pad_ref, shifted_ref
    ):
        mark_ref[...] = jnp.zeros_like(mark_ref)
        fill(pad_ref, shifted_ref, low_ref, mid_ref, high_ref)
        for lane in range(0, tile, LANES):
            at = slice(lane, lane + LANES)
            conv = jnp.zeros((rows, LANES), F32)
            for k in range(count):
                conv = conv + taps_ref[k : k + 1, at] * tap_rows(shifted_ref, first + k, rows, at)
            conv_ref[:, at] = conv
            gated = conv / (1.0 + jnp.exp(-conv))
            gated_ref[:, at] = gated.astype(BF)
            turned_ref[at, :] = gated.T.astype(BF)

    edge, body_spec = tap_specs(rows, tile)
    return pl.pallas_call(
        kernel,
        grid=(width // tile,),
        out_shape=(
            jax.ShapeDtypeStruct((rows, width), F32),
            jax.ShapeDtypeStruct((rows, width), BF),
            jax.ShapeDtypeStruct((width, rows), BF),
            jax.ShapeDtypeStruct((8, LANES), F32),
        ),
        in_specs=[edge, body_spec, edge, pl.BlockSpec((count, tile), lambda j: (0, j))],
        out_specs=(
            body_spec,
            body_spec,
            pl.BlockSpec((tile, rows), lambda j: (j, 0)),
            pl.BlockSpec((8, LANES), lambda j: (0, 0)),
        ),
        scratch_shapes=pad_scratch(rows, tile),
        compiler_params=pltpu.CompilerParams(vmem_limit_bytes=VMEM_BYTES),
        cost_estimate=CHEAP,
        name="convolve",
    )(low, frames, high, taps)


def convolve_back(low, dconv, high, taps, dmixed):
    rows, width = dconv.shape
    count = taps.shape[0]
    last = EDGE + (count - 1) // 2
    tile = channel_tile(width)

    def kernel(low_ref, mid_ref, high_ref, taps_ref, dmixed_ref, out_ref, pad_ref, shifted_ref):
        fill(pad_ref, shifted_ref, low_ref, mid_ref, high_ref)
        for lane in range(0, tile, LANES):
            at = slice(lane, lane + LANES)
            back = dmixed_ref[:, at].astype(F32)
            for k in range(count):
                back = back + taps_ref[k : k + 1, at] * tap_rows(shifted_ref, last - k, rows, at)
            out_ref[:, at] = back.astype(BF)

    edge, body_spec = tap_specs(rows, tile)
    return pl.pallas_call(
        kernel,
        grid=(width // tile,),
        out_shape=jax.ShapeDtypeStruct((rows, width), BF),
        in_specs=[edge, body_spec, edge, pl.BlockSpec((count, tile), lambda j: (0, j)), body_spec],
        out_specs=body_spec,
        scratch_shapes=pad_scratch(rows, tile),
        compiler_params=pltpu.CompilerParams(vmem_limit_bytes=VMEM_BYTES),
        cost_estimate=CHEAP,
        name="convolve_back",
    )(low, dconv, high, taps, dmixed)


def gate_back(dmixed, pw_full, conv, low, frames, high, count, earlier):
    rows, width = dmixed.shape
    first = EDGE - (count - 1) // 2
    tile = channel_tile(width)
    held = -(-count // 16) * 16

    def kernel(
        dmixed_ref, pw_ref, conv_ref, low_ref, mid_ref, high_ref, _, dconv_ref, taps_ref, pad_ref,
        shifted_ref,
    ):
        fill(pad_ref, shifted_ref, low_ref, mid_ref, high_ref)
        dgated = lax.dot_general(
            dmixed_ref[...], pw_ref[...], (((1,), (1,)), ((), ())), preferred_element_type=F32
        )
        conv = conv_ref[...]
        sig = 1.0 / (1.0 + jnp.exp(-conv))
        dconv_ref[...] = (dgated * sig * (1.0 + conv * (1.0 - sig))).astype(BF)
        taps_ref[...] = jnp.zeros_like(taps_ref)
        for lane in range(0, tile, LANES):
            at = slice(lane, lane + LANES)
            dconv = dconv_ref[:, at].astype(F32)
            for k in range(count):
                term = dconv * tap_rows(shifted_ref, first + k, rows, at)
                taps_ref[k : k + 1, at] = jnp.sum(term, axis=0, keepdims=True)

    edge, body_spec = tap_specs(rows, tile)
    return pl.pallas_call(
        kernel,
        grid=(width // tile,),
        out_shape=(
            jax.ShapeDtypeStruct((rows, width), BF),
            jax.ShapeDtypeStruct((held, width), F32),
        ),
        in_specs=[
            pl.BlockSpec((rows, width), lambda j: (0, 0)),
            pl.BlockSpec((tile, width), lambda j: (j, 0)),
            body_spec,
            edge,
            body_spec,
            edge,
            pl.BlockSpec(memory_space=pl.ANY),
        ],
        out_specs=(body_spec, pl.BlockSpec((held, tile), lambda j: (0, j))),
        scratch_shapes=pad_scratch(rows, tile),
        compiler_params=pltpu.CompilerParams(vmem_limit_bytes=VMEM_BYTES),
        cost_estimate=pl.CostEstimate(
            flops=6 * 10**9, bytes_accessed=44 * 10**6, transcendentals=0
        ),
        name="gate_back",
    )(dmixed, pw_full, conv, low, frames, high, earlier)


def head_terms(left_own, left_other, right_own, right_other, earlier):
    width = left_own[0].shape[1]
    depth, vocab = right_own.shape
    split = left_own[0].shape[0]
    tile = channel_tile(width)

    def kernel(near_a, far_a, near_b, far_b, ra_ref, rb_ref, _, out_ref):
        lhs = (((0,), (0,)), ((), ()))
        term = jnp.zeros(out_ref.shape, F32)
        for near, far, right in ((near_a, far_a, ra_ref), (near_b, far_b, rb_ref)):
            term += lax.dot_general(near[...], right[:split], lhs, preferred_element_type=F32)
            term += lax.dot_general(far[...], right[split:], lhs, preferred_element_type=F32)
        out_ref[...] = term.astype(BF)

    near = pl.BlockSpec((split, tile), lambda j: (0, j))
    far = pl.BlockSpec((depth - split, tile), lambda j: (0, j))
    right = pl.BlockSpec((depth, vocab), lambda j: (0, 0))
    return pl.pallas_call(
        kernel,
        grid=(width // tile,),
        out_shape=jax.ShapeDtypeStruct((width, vocab), BF),
        in_specs=[near, far, near, far, right, right, pl.BlockSpec(memory_space=pl.ANY)],
        out_specs=pl.BlockSpec((tile, vocab), lambda j: (j, 0)),
        compiler_params=pltpu.CompilerParams(vmem_limit_bytes=VMEM_BYTES),
        cost_estimate=pl.CostEstimate(
            flops=13 * 10**9, bytes_accessed=40 * 10**6, transcendentals=0
        ),
        name="head_terms",
    )(*left_own, *left_other, right_own, right_other, earlier)


def logits_and_stats(mixed, head, other):
    rows, width = mixed.shape
    vocab = head.shape[1]
    tile = min(LOGIT_TILE, vocab)
    steps = vocab // tile

    def kernel(x_ref, a_ref, b_ref, la_ref, lb_ref, stats_ref, top_ref, total_ref):
        step = pl.program_id(0)

        @pl.when(step == 0)
        def _():
            top_ref[...] = jnp.full_like(top_ref, -jnp.inf)
            total_ref[...] = jnp.zeros_like(total_ref)

        la_ref[...] = jnp.dot(x_ref[...], a_ref[...], preferred_element_type=F32)
        lb_ref[...] = jnp.dot(x_ref[...], b_ref[...], preferred_element_type=F32)
        parts = [
            ref[:, lane : lane + LANES] for ref in (la_ref, lb_ref) for lane in range(0, tile, LANES)
        ]
        old = top_ref[...]
        new = old
        for part in parts:
            new = jnp.maximum(new, part)
        total = total_ref[...] * jnp.exp(old - new)
        for part in parts:
            total = total + jnp.exp(part - new)
        top_ref[...] = new
        total_ref[...] = total

        @pl.when(step == steps - 1)
        def _():
            tops, totals = new.T, total.T
            top = jnp.max(tops, axis=0, keepdims=True)
            total_row = jnp.sum(totals * jnp.exp(tops - top), axis=0, keepdims=True)
            row = lax.broadcasted_iota(jnp.int32, (8, rows), 0)
            stats_ref[...] = jnp.where(row == 0, top, total_row)

    columns = pl.BlockSpec((width, tile), lambda j: (0, j))
    made = pl.BlockSpec((rows, tile), lambda j: (0, j))
    return pl.pallas_call(
        kernel,
        grid=(steps,),
        out_shape=(
            jax.ShapeDtypeStruct((rows, vocab), F32),
            jax.ShapeDtypeStruct((rows, vocab), F32),
            jax.ShapeDtypeStruct((8, rows), F32),
        ),
        in_specs=[pl.BlockSpec((rows, width), lambda j: (0, 0)), columns, columns],
        out_specs=(made, made, pl.BlockSpec((8, rows), lambda j: (0, 0))),
        scratch_shapes=[pltpu.VMEM((rows, 128), F32), pltpu.VMEM((rows, 128), F32)],
        compiler_params=pltpu.CompilerParams(vmem_limit_bytes=VMEM_BYTES),
        cost_estimate=pl.CostEstimate(flops=0, bytes_accessed=0, transcendentals=0),
        name="logits",
    )(mixed, head, other)


def logit_gradients(firsts, near, far, stats, labels):
    chips = len(stats)
    rows, vocab = far[0].shape
    tile = min(LOGIT_TILE, vocab)

    def kernel(*refs):
        first_ref = refs[0]
        logit_refs = [refs[1 + 2 * m : 3 + 2 * m] for m in range(chips)]
        stat_refs = refs[1 + 2 * chips : 1 + 3 * chips]
        label_refs = refs[1 + 3 * chips : 1 + 4 * chips]
        own_ref, other_ref, columns_ref = refs[1 + 4 * chips :]
        step = pl.program_id(0)

        @pl.when(step == 0)
        def _():
            for m in range(chips):
                tops, totals = [], []
                for o in range(chips):
                    at = m ^ o
                    tops.append(stat_refs[o][at : at + 1, :])
                    totals.append(stat_refs[o][chips + at : chips + at + 1, :])
                top = tops[0]
                for t in tops[1:]:
                    top = jnp.maximum(top, t)
                total = sum(s * jnp.exp(t - top) for s, t in zip(totals, tops))
                values = jnp.concatenate(
                    [
                        top,
                        1.0 / total,
                        label_refs[m][0:1, :],
                        label_refs[m][1:2, :],
                        jnp.zeros((124, rows), F32),
                    ],
                    axis=0,
                )
                columns_ref[m] = values.T

        entries = lax.broadcasted_iota(jnp.int32, (rows, tile), 1) + step * tile
        for m in range(chips):
            columns = columns_ref[m]
            top, inverse = columns[:, 0:1], columns[:, 1:2]
            target = columns[:, 2:3].astype(jnp.int32)
            weight = columns[:, 3:4]
            for k, out_ref in enumerate((own_ref, other_ref)):
                probs = jnp.exp(logit_refs[m][k][...] - top) * inverse
                hit = (entries == target - first_ref[k]).astype(F32)
                out_ref[m * rows : (m + 1) * rows, :] = (weight * (probs - hit)).astype(BF)

    def block(index):
        return pl.BlockSpec((rows, tile), lambda j: (index, j))

    made = pl.BlockSpec((chips * rows, tile), lambda j: (0, j))
    return pl.pallas_call(
        kernel,
        grid=(vocab // tile,),
        out_shape=(
            jax.ShapeDtypeStruct((chips * rows, vocab), BF),
            jax.ShapeDtypeStruct((chips * rows, vocab), BF),
        ),
        in_specs=[pl.BlockSpec(memory_space=pltpu.SMEM)]
        + [block(m) for m in range(chips - 1) for _ in range(2)]
        + [block(0)] * 2
        + [pl.BlockSpec((2 * chips, rows), lambda j: (0, 0))] * chips
        + [pl.BlockSpec((2, rows), lambda j: (0, 0))] * chips,
        out_specs=(made, made),
        scratch_shapes=[pltpu.VMEM((chips, rows, 128), F32)],
        compiler_params=pltpu.CompilerParams(vmem_limit_bytes=VMEM_BYTES),
        cost_estimate=pl.CostEstimate(flops=0, bytes_accessed=0, transcendentals=0),
        name="dlogits",
    )(firsts, *(list(near) * (chips - 1)), *far, *stats, *labels)


def body(frames, conv_kernel, pw_weight, head_weight, targets, frame_weight):
    frames = frames[0]
    rows, width = frames.shape
    taps = conv_kernel.shape[0]
    seqs = lax.axis_size("seq")
    count = lax.axis_size("fsdp")
    chips = count // 2
    me = lax.axis_index("fsdp")
    chip = me // 2
    core = me % 2
    low, high = halo_edges(frames[:EDGE], frames[-EDGE:])
    conv, gated, turned, mark = convolve(low, frames, high, conv_kernel)
    shard = pw_weight.shape[0]
    pieces, places = [], []
    gathered = gather_pieces(pw_weight, mark)
    for piece, m, first in gathered:
        pieces += [piece, swap(piece, 1)]
        places += [(me ^ (2 * m)) * shard + first, (me ^ (2 * m + 1)) * shard + first]
    places = jnp.stack(places).astype(jnp.int32)
    head_other = swap(head_weight, 1)

    mixed, pw_full = project(gated, frames, pieces, places)
    labels = jnp.stack([targets[0].astype(F32), frame_weight[0].astype(F32)])
    all_labels = [labels] + [swap(labels, 2 * m) for m in range(1, chips)]

    piece = width // (seqs * count)
    gated_t = turned.reshape(seqs, chips, 2, piece, rows)
    gated_t = jnp.stack(
        [lax.dynamic_index_in_dim(gated_t, chip ^ m, 1, keepdims=False) for m in range(chips)]
    )
    gated_own = lax.dynamic_index_in_dim(gated_t, core, 2, keepdims=False)
    gated_sent = lax.dynamic_index_in_dim(gated_t, 1 - core, 2, keepdims=False)
    gated_got = swap(gated_sent, 1)
    gated_pair = jnp.concatenate([gated_own, gated_got], axis=-1)

    weights = (head_weight, head_other)
    vocab = head_weight.shape[1]
    pairs, tops, totals = [], [], []

    def near_logits(block):
        own, other, stats = logits_and_stats(block, *weights)
        pairs.append((own, other))
        tops.append(stats[0].reshape(-1, rows))
        totals.append(stats[1].reshape(-1, rows))
        return (stats,)

    near_own, far_own = gather_rows(mixed, (gated_got,), near_logits)
    pair = [jnp.dot(far_own, w, preferred_element_type=F32) for w in weights]
    top = jnp.maximum(jnp.max(pair[0], axis=1), jnp.max(pair[1], axis=1))
    total = sum(jnp.sum(jnp.exp(l - top[:, None]), axis=1) for l in pair)
    pairs.append(pair)
    tops.append(top.reshape(-1, rows))
    totals.append(total.reshape(-1, rows))
    near_other = swap(near_own, 1)
    far_other = swap(far_own, 1)
    packed = jnp.concatenate(tops + totals)
    got = [packed] + [swap(packed, 2 * m) for m in range(1, chips)]
    firsts = jnp.stack([me * vocab, (me ^ 1) * vocab]).astype(jnp.int32)
    right_own, right_sent = logit_gradients(firsts, pairs[0], pairs[1], got, all_labels)
    right_other = swap(right_sent, 1)

    def back_head(m):
        rhs = (((1,), (1,)), ((), ()))
        at = slice(m * rows, (m + 1) * rows)
        return lax.dot_general(
            right_own[at], head_weight, rhs, preferred_element_type=F32
        ) + lax.dot_general(right_sent[at], head_other, rhs, preferred_element_type=F32)

    terms = []

    def while_dmixed_travels(_, sent):
        terms.append(
            head_terms((near_own, far_own), (near_other, far_other), right_own, right_other, sent)
        )
        return (), (terms[0],)

    dmixed, _, _ = scatter_and_finish(
        back_head, lambda m: (back_head(m), 0), chips, (), while_dmixed_travels, BF
    )
    head_grad = lax.psum_scatter(terms[0], "seq", scatter_dimension=0, tiled=True).astype(F32)

    dmixed_pair = jnp.concatenate([dmixed, swap(dmixed, 1)], axis=0)
    pw_term = jnp.dot(
        gated_pair.reshape(-1, 2 * rows), dmixed_pair, preferred_element_type=F32
    )
    dconv, kernel_rows = gate_back(
        dmixed, pw_full, conv, low, frames, high, taps, pw_term[:8, :LANES]
    )
    size = seqs * piece
    first = core == 0
    share = kernel_rows.shape[0] // 2

    def while_pw_travels(kept, _):
        dlow, dhigh = halo_edges(*kept[:2])
        low_taps, high_taps = kept[2][:share], kept[2][share:]
        part = jnp.where(first, low_taps, high_taps) + swap(
            jnp.where(first, high_taps, low_taps), 1
        )
        terms = [part] + [
            lax.ppermute(part, "seq", [(i, i ^ m) for i in range(seqs)]) for m in range(1, seqs)
        ]
        while len(terms) > 1:
            terms = [terms[n] + terms[n + 1] for n in range(0, len(terms), 2)]
        total = terms[0]
        backs.append(convolve_back(dlow, dconv, dhigh, conv_kernel, dmixed))
        return (total,), (backs[0],)

    backs = []
    pw_sum, _, (kernel_sum,) = scatter_and_finish(
        lambda m: pw_term[m * size : (m + 1) * size],
        lambda m: (pw_term, m),
        chips,
        (
            (dconv, EDGE, 0),
            (dconv, EDGE, rows // EDGE - 1),
            (kernel_rows, kernel_rows.shape[0], 0),
        ),
        while_pw_travels,
        F32,
    )
    back = backs[0]
    pw_sum = pw_sum.reshape(seqs, piece, width)
    here = lax.axis_index("seq")

    def shard_of(m):
        return lax.dynamic_index_in_dim(pw_sum, here ^ m, 0, keepdims=False)

    pw_grad = shard_of(0)
    for m in range(1, seqs):
        moved = lax.ppermute(
            shard_of(m).astype(BF), "seq", [(i, i ^ m) for i in range(seqs)]
        )
        pw_grad = pw_grad + moved.astype(F32)

    mask = 2
    while mask < count:
        kernel_sum = kernel_sum + swap(kernel_sum, mask)
        mask *= 2
    kernel_got = swap(kernel_sum, 1)
    kernel_grad = jnp.concatenate(
        [
            jnp.where(first, kernel_sum, kernel_got),
            jnp.where(first, kernel_got, kernel_sum)[: taps - share],
        ],
        axis=0,
    )
    return (back[None], kernel_grad, pw_grad, head_grad)


def solution(mesh):
    return jax.shard_map(
        body,
        mesh=mesh,
        in_specs=(
            P("fsdp", "seq", None),
            P(),
            P("fsdp", None),
            P(None, "fsdp"),
            P("fsdp", "seq"),
            P("fsdp", "seq"),
        ),
        out_specs=(P("fsdp", "seq", None), P(), P(("seq", "fsdp"), None), P("seq", "fsdp")),
        check_vma=False,
    )
```
